512 devices in a mesh: head: 16 (over x_hi, y, core), ctx: 32 (over x_lo, z).
Axes of the slice: x: 4 (x_hi: 2, x_lo: 2; x = x_hi * 2 + x_lo), y: 4, z: 16, core: 2. Of those that a mesh axis runs over, the one named last changes fastest.
Arguments:
- queries: bfloat16 [64, 8192, 128], P('head', 'ctx'), may hold values from -8 to 8
- key_heads: bfloat16 [4, 8192, 128], P(None, 'ctx'), may hold values from -8 to 8
- value_heads: bfloat16 [4, 8192, 128], P(None, 'ctx'), may hold values from -6 to 6
- doc_lengths: int32 [16], replicated, may hold values from 1 to 4096, 8192 in all
- span_order: int32 [64], replicated, may hold values from 0 to 63, each once
Outputs:
- attended: bfloat16 [64, 8192, 128], P('head', 'ctx')
The draws below stay inside these ranges and needn't reach their ends.
All inputs are finite; a program needn't handle non-finite values.
Results may differ from the reference program's by a relative error of at most 0.005.
Values may be sent and summed in bfloat16 or wider, within the bound.
A program may use at most 128 MiB of HBM per device.

```python
import math
import jax
import jax.numpy as jnp
import numpy as np
from jax import lax

DH = 128
GROUP = 16
HQ = 64
KVH = 4
SPAN = 128
L = 8192
NCH = 64
NDOC = 16
MOST = 4096


def draw_queries(key, part):
    drawn = jnp.clip(jax.random.normal(jax.random.fold_in(key, 3), (HQ, L, DH), jnp.float32), -4.0, 4.0)
    return drawn.astype(jnp.bfloat16)


def draw_key_heads(key, part):
    drawn = jnp.clip(jax.random.normal(jax.random.fold_in(key, 4), (KVH, L, DH), jnp.float32), -4.0, 4.0)
    return drawn.astype(jnp.bfloat16)


def block_levels(rng, shape, shards, smallest, largest):
    gain = 1.0
    for dim, parts in shards:
        draws = jax.random.uniform(jax.random.fold_in(jax.random.fold_in(rng, 6), dim), (parts,), jnp.float32, smallest / len(shards), largest / len(shards))
        gain = gain * jnp.repeat(jnp.exp(draws), shape[dim] // parts).reshape((-1,) + (1,) * (len(shape) - 1 - dim))
    return gain


def split_up(amount, total, bound, slope):
    portions = [(1 << 20) // math.isqrt(rank ** slope) + 1 for rank in range(2, amount + 1)]
    rest, counts = total - bound - (amount - 1), [1] * (amount - 1)
    while rest > 0:
        movable = [i for i in range(amount - 1) if counts[i] < bound]
        whole, remaining = sum([portions[i] for i in movable]), rest
        for i in movable:
            extra = min(bound - counts[i], max(1, remaining * portions[i] // whole), rest)
            counts[i] = counts[i] + extra
            rest = rest - extra
    return np.array([bound] + counts)


def ragged_sizes(stream_key, count, total, bound, skew):
    if count == 2:
        one = jax.random.randint(stream_key, (), max(1, total - bound), min(bound, total - 1) + 1)
        return jnp.stack([one, total - one])
    lengths = jnp.asarray(split_up(count, total, bound, skew), jnp.int32)
    pairs = (count - 1) // 2
    giver, taker = lengths[1:1 + 2 * pairs:2], lengths[2:2 + 2 * pairs:2]
    slack = jnp.minimum(giver - 1, bound - taker)
    shifted = jax.random.randint(jax.random.fold_in(stream_key, 1), (pairs,), 0, 1 << 20) % (slack + 1)
    lengths = lengths.at[1:1 + 2 * pairs:2].set(giver - shifted).at[2:2 + 2 * pairs:2].set(taker + shifted)
    return lengths[jax.random.permutation(jax.random.fold_in(stream_key, 2), count)]


def centred(key, dims, spread, bound, cuts=(), kind=jnp.bfloat16):
    result = jax.random.normal(key, dims, jnp.float32) * spread
    if len(cuts) > 0:
        result = block_levels(key, dims, cuts, -0.22, 0.18) * result
    return jnp.clip(result, min=-bound, max=bound).astype(kind)


def setup_inputs(seed: int = 0) -> dict:
    splits = jax.random.split(jax.random.key(seed), 6)
    return {
        "queries": draw_queries(jax.random.fold_in(splits[5], 71), 0),
        "key_heads": draw_key_heads(jax.random.fold_in(splits[5], 71), 0),
        "value_heads": centred(splits[2], (KVH, L, DH), 1.0, 6.0, ((1, 32),)),
        "doc_lengths": ragged_sizes(splits[3], NDOC, L, MOST, 2).astype(jnp.int32),
        "span_order": jax.random.permutation(splits[4], NCH).astype(jnp.int32),
    }


masked_score = -1e+30

def reference(queries, key_heads, value_heads, doc_lengths, span_order):
    row_ids = jnp.arange(L, dtype=jnp.int32)
    positions = span_order[row_ids // SPAN] * SPAN + row_ids % SPAN
    doc_ends = jnp.cumsum(doc_lengths)
    doc_ids = lax.optimization_barrier(jnp.sum((positions[:, None] >= doc_ends[None, :-1]).astype(jnp.int32), axis=1))
    block_rows = math.gcd(L, 1024)
    block_count = L // block_rows
    scale = 1.0 / math.sqrt(DH)

    def one_block(index):
        head = (index // block_count).astype(jnp.int32)
        first_row = (index % block_count * block_rows).astype(jnp.int32)
        head_rows = lax.dynamic_index_in_dim(queries, head, 0, keepdims=False)
        query_block = lax.dynamic_slice_in_dim(head_rows, first_row, block_rows, 0).astype(jnp.float32)
        group = (head // GROUP).astype(jnp.int32)
        group_keys = lax.dynamic_index_in_dim(key_heads, group, 0, keepdims=False).astype(jnp.float32)
        group_values = lax.dynamic_index_in_dim(value_heads, group, 0, keepdims=False).astype(jnp.float32)
        query_pos = lax.dynamic_slice_in_dim(positions, first_row, block_rows, 0)
        query_doc = lax.dynamic_slice_in_dim(doc_ids, first_row, block_rows, 0)
        allowed = (query_doc[:, None] == doc_ids[None, :]) & (positions[None, :] <= query_pos[:, None])
        scores = jnp.dot(query_block, group_keys.T, precision=lax.Precision.HIGHEST) * scale
        scores = jnp.where(allowed, scores, masked_score)
        row_max = lax.optimization_barrier(jnp.max(scores, axis=1))
        weights = jnp.where(allowed, jnp.exp(scores - row_max[:, None]), 0.0)
        weight_sum = lax.optimization_barrier(jnp.sum(weights, axis=1))
        rounded = lax.optimization_barrier(weights.astype(jnp.bfloat16))
        mixed = jnp.dot(rounded.astype(jnp.float32), group_values, precision=lax.Precision.HIGHEST)
        return (mixed / weight_sum[:, None]).astype(jnp.bfloat16)
    blocks = lax.map(one_block, jnp.arange(HQ * block_count, dtype=jnp.int32))
    return blocks.reshape(HQ, L, DH)
```

```python
import math

import jax
import jax.numpy as jnp
from jax import lax
from jax.experimental import pallas as pl
from jax.experimental.pallas import tpu as pltpu
from jax.sharding import PartitionSpec as P

MESH = pl.DeviceIdType.MESH
SPAN = 128
DH = 128
DOCS = 16
SPANS = 64
RING = 16
BIG = 131072.0
FACTOR = math.log2(math.e) / math.sqrt(DH)
ONES = 16
COMM = True
COMPUTE = True


def kernel(q_ref, k_ref, v_ref, lens_ref, order_ref, out_ref,
           buf, ext, qx, vtmp, acc, top, send_sem, recv_sem, local_sem):
    head = lax.axis_index("head")
    ctx = lax.axis_index("ctx")
    core = lax.rem(head, 2)
    y_lo = lax.rem(head // 2, 2)
    x_lo = ctx // RING
    z = lax.rem(ctx, RING)
    group = head // 4

    own = 2 * ctx
    local = [
        pltpu.make_async_copy(k_ref.at[group], buf.at[0, pl.ds(own, 2)], local_sem.at[0]),
        pltpu.make_async_copy(v_ref.at[group], vtmp, local_sem.at[1]),
        pltpu.make_async_copy(q_ref, qx.at[:, :, pl.ds(0, DH)], local_sem.at[2]),
    ]
    for copy in local:
        copy.start()

    other_x = 1 - x_lo
    to_up = {"ctx": x_lo * RING + lax.rem(z + 1, RING)}
    to_down = {"ctx": x_lo * RING + lax.rem(z + RING - 1, RING)}
    to_x = {"ctx": other_x * RING + z}
    to_y = {"head": head + 2 - 4 * y_lo}
    to_core = {"head": head + 1 - 2 * core}

    if COMM:
        barrier = pltpu.get_barrier_semaphore()
        for device in (to_up, to_down, to_x, to_y, to_core):
            pl.semaphore_signal(barrier, inc=1, device_id=device, device_id_type=MESH)

    def unit(kv, span, device):
        return pltpu.make_async_remote_copy(
            src_ref=buf.at[kv, span],
            dst_ref=buf.at[kv, span],
            send_sem=send_sem,
            recv_sem=recv_sem.at[kv, span],
            device_id=device,
            device_id_type=MESH,
        )

    def send(kv, span, device):
        if COMM:
            unit(kv, span, device).start()

    def arrived(kv, span):
        if COMM:
            unit(kv, span, to_core).wait_recv()

    def first(x, level, side):
        return 2 * (x * RING + lax.rem(level + RING, RING)) + (y_lo if side == 0 else 1 - y_lo)

    def along(t, side, directions, onward):
        for direction in directions:
            span = first(x_lo, z - direction * t, side)
            arrived(core, span)
            if direction in onward:
                send(core, span, to_up if direction == 1 else to_down)
            if side == 0:
                send(core, span, to_x)
            send(core, span, to_core)

    def levels(t):
        return [z - t, z + t]

    def from_x(places):
        for level in places:
            span = first(other_x, level, 0)
            arrived(core, span)
            send(core, span, to_y)
            send(core, span, to_core)

    def from_y(places):
        for level in places:
            span = first(other_x, level, 1)
            arrived(core, span)
            send(core, span, to_core)

    def ready(x, places):
        for level in places:
            for side in (0, 1):
                arrived(1 - core, first(x, level, side))

    def attend(slots, own_slot=False):
        if not COMPUTE:
            return
        spans = [2 * (x * RING + lax.rem(level + RING, RING)) + j for x, level in slots for j in (0, 1)]
        keys = jnp.concatenate(
            [jnp.concatenate([buf[0, s], ext[s]], axis=1) for s in spans], axis=0
        )
        values = jnp.concatenate([buf[1, s] for s in spans], axis=1)
        values = jnp.concatenate(
            [values, jnp.ones((ONES, values.shape[1]), jnp.bfloat16)], axis=0
        )
        for h in range(4):
            scores = lax.dot_general(
                keys, qx[h], (((1,), (1,)), ((), ())), preferred_element_type=jnp.float32
            )
            if own_slot:
                key_row = lax.broadcasted_iota(jnp.int32, scores.shape, 0)
                query_row = lax.broadcasted_iota(jnp.int32, scores.shape, 1)
                later = (key_row > query_row) & (
                    (key_row >= SPAN) == (query_row >= SPAN)
                )
                scores = jnp.where(later, -BIG, scores)
            scores = scores * FACTOR
            highest = jnp.max(scores, axis=0, keepdims=True)
            if own_slot:
                new_top = highest
            else:
                old_top = top[h:h + 1, :]
                new_top = jnp.maximum(old_top, highest)
            weights = jnp.exp2(scores - new_top).astype(jnp.bfloat16)
            mixed = lax.dot_general(
                values, weights, (((1,), (0,)), ((), ())), preferred_element_type=jnp.float32
            )
            if own_slot:
                acc[h] = mixed
            else:
                acc[h] = acc[h] * jnp.exp2(old_top - new_top) + mixed
            top[h:h + 1, :] = new_top

    local[1].wait()
    for j in (0, 1):
        block = vtmp[j * SPAN:(j + 1) * SPAN, :].astype(jnp.float32)
        buf[1, own + j] = block.T.astype(jnp.bfloat16)
    local[0].wait()
    if COMM:
        pl.semaphore_wait(barrier, 5)
    for side in (0, 1):
        span = first(x_lo, z, side)
        send(core, span, to_up)
        send(core, span, to_down)
        if side == 0:
            send(core, span, to_x)

    lane = lax.broadcasted_iota(jnp.int32, (1, DH), 1)
    opens = jnp.where(lane < SPANS, lane * SPAN, 1 << 20)
    closes = jnp.where(lane < SPANS, lane * SPAN + SPAN, 1 << 20)
    end = jnp.int32(0)
    for d in range(DOCS):
        opens = jnp.where(lane == SPANS + d, end, opens)
        end = end + lens_ref[d]
        closes = jnp.where(lane == SPANS + d, end if d < DOCS - 1 else 1 << 20, closes)

    def inside(span):
        position = order_ref[span] * SPAN + lax.broadcasted_iota(jnp.int32, (SPAN, 1), 0)
        return (position >= opens) & (position < closes)

    def marks(s, carry):
        ext[s] = jnp.where(inside(s), 1.0, 0.0).astype(jnp.bfloat16)
        return carry

    for j in (0, 1):
        outside = jnp.where(inside(own + j), 0.0, -BIG)
        after = jnp.where(lane > order_ref[own + j], -BIG, 0.0)
        side_q = jnp.where(lane < SPANS, after, jnp.where(lane < SPANS + DOCS, outside, 0.0))
        for h in range(4):
            qx[h, j * SPAN:(j + 1) * SPAN, DH:] = side_q.astype(jnp.bfloat16)
    lax.fori_loop(0, SPANS, marks, 0, unroll=4)
    local[2].wait()

    along(1, 0, (1, -1), (1, -1))
    along(1, 1, (1, -1), (1, -1))
    attend([(x_lo, z)], own_slot=True)

    def turn(t, carry):
        @pl.when(t <= 6)
        def _():
            along(t, 0, (1, -1), (1, -1))

        @pl.when(t == 7)
        def _():
            along(t, 0, (1, -1), (1,))

        @pl.when(t == 8)
        def _():
            along(t, 0, (1,), ())

        @pl.when(t <= 8)
        def _():
            from_x(levels(t - 1))
            ready(x_lo, levels(t - 1))
            attend([(x_lo, level) for level in levels(t - 1)])

        @pl.when(t <= 6)
        def _():
            along(t, 1, (1, -1), (1, -1))

        @pl.when(t == 7)
        def _():
            along(t, 1, (1, -1), (-1,))

        @pl.when(t == 8)
        def _():
            along(t, 1, (-1,), ())

        @pl.when(t == 9)
        def _():
            from_x([z - 8])

        @pl.when((t >= 3) & (t <= 9))
        def _():
            from_y(levels(t - 2))

        @pl.when(t == 10)
        def _():
            from_y([z - 8])

        @pl.when(t >= 4)
        def _():
            ready(other_x, levels(t - 3))
            attend([(other_x, level) for level in levels(t - 3)])

        @pl.when(t == 2)
        def _():
            from_x([z])

        @pl.when(t == 3)
        def _():
            from_y([z])
            ready(other_x, [z])
            attend([(other_x, z)])

        return carry

    lax.fori_loop(2, 11, turn, 0)
    ready(x_lo, [z - 8])
    ready(other_x, [z - 8])
    attend([(x_lo, z - 8), (other_x, z - 8)])

    if COMPUTE:
        for h in range(4):
            result = acc[h, :DH, :] / acc[h, DH:DH + 1, :]
            out_ref[h] = result.T.astype(jnp.bfloat16)
    else:
        for h in range(4):
            out_ref[h] = (buf[0, 2 * h].astype(jnp.float32) + buf[1, 2 * h + 9]).astype(jnp.bfloat16)[:1, :] + jnp.zeros((256, DH), jnp.bfloat16)
    if COMM:
        pltpu.make_async_copy(buf.at[:, pl.ds(0, 62)], buf.at[:, pl.ds(0, 62)], send_sem).wait()


def body(queries, key_heads, value_heads, doc_lengths, span_order):
    heads, rows, _ = queries.shape
    shape = (key_heads.shape[0], 2, SPAN, DH)
    return pl.pallas_call(
        kernel,
        out_shape=jax.ShapeDtypeStruct(queries.shape, jnp.bfloat16),
        in_specs=[
            pl.BlockSpec(memory_space=pl.ANY),
            pl.BlockSpec(memory_space=pl.ANY),
            pl.BlockSpec(memory_space=pl.ANY),
            pl.BlockSpec(memory_space=pltpu.SMEM),
            pl.BlockSpec(memory_space=pltpu.SMEM),
        ],
        out_specs=pl.BlockSpec(memory_space=pltpu.VMEM),
        scratch_shapes=[
            pltpu.VMEM((2, SPANS, SPAN, DH), jnp.bfloat16),
            pltpu.VMEM((SPANS, SPAN, DH), jnp.bfloat16),
            pltpu.VMEM((heads, rows, 2 * DH), jnp.bfloat16),
            pltpu.VMEM((rows, DH), jnp.bfloat16),
            pltpu.VMEM((heads, DH + ONES, rows), jnp.float32),
            pltpu.VMEM((8, rows), jnp.float32),
            pltpu.SemaphoreType.DMA,
            pltpu.SemaphoreType.DMA((2, SPANS)),
            pltpu.SemaphoreType.DMA((3,)),
        ],
        compiler_params=pltpu.CompilerParams(
            collective_id=0 if COMM else None, has_side_effects=True, vmem_limit_bytes=48 * 2**20
        ),
        cost_estimate=pl.CostEstimate(
            flops=4 * heads * rows * SPANS * SPAN * DH,
            bytes_accessed=2**20,
            transcendentals=heads * rows * SPANS * SPAN,
        ),
    )(queries, key_heads.reshape(shape), value_heads, doc_lengths, span_order)


def solution(mesh):
    return jax.shard_map(
        body,
        mesh=mesh,
        in_specs=(P("head", "ctx", None), P(None, "ctx", None), P(None, "ctx", None), P(), P()),
        out_specs=P("head", "ctx", None),
        check_vma=False,
    )
```

```python
import math

import jax
import jax.numpy as jnp
from jax import lax
from jax.experimental import pallas as pl
from jax.experimental.pallas import tpu as pltpu
from jax.sharding import PartitionSpec as P

MESH = pl.DeviceIdType.MESH
SPAN = 128
DH = 128
DOCS = 16
SPANS = 64
RING = 16
BIG = 131072.0
FACTOR = math.log2(math.e) / math.sqrt(DH)
ONES = 16
COMM = True
COMPUTE = True


def kernel(q_ref, k_ref, v_ref, lens_ref, order_ref, out_ref,
           buf, ext, qx, qtmp, vtmp, acc, top, send_sem, recv_sem, local_sem):
    head = lax.axis_index("head")
    ctx = lax.axis_index("ctx")
    core = lax.rem(head, 2)
    y_lo = lax.rem(head // 2, 2)
    x_lo = ctx // RING
    z = lax.rem(ctx, RING)
    group = head // 4
    own = 2 * ctx
    other_x = 1 - x_lo

    local = [
        pltpu.make_async_copy(k_ref.at[group], buf.at[0, pl.ds(own, 2)], local_sem.at[0]),
        pltpu.make_async_copy(v_ref.at[group], vtmp, local_sem.at[1]),
        pltpu.make_async_copy(q_ref, qtmp, local_sem.at[2]),
    ]
    for copy in local:
        copy.start()

    def along(distance):
        return {"ctx": x_lo * RING + lax.rem(z + distance + RING, RING)}

    to_x = {"ctx": other_x * RING + z}
    to_y = {"head": head + 2 - 4 * y_lo}
    to_core = {"head": head + 1 - 2 * core}

    if COMM:
        barrier = pltpu.get_barrier_semaphore()
        for device in (along(1), along(-1), along(2), along(-2), to_x, to_y, to_core):
            pl.semaphore_signal(barrier, inc=1, device_id=device, device_id_type=MESH)

    def unit(kv, span, device):
        return pltpu.make_async_remote_copy(
            src_ref=buf.at[kv, span],
            dst_ref=buf.at[kv, span],
            send_sem=send_sem,
            recv_sem=recv_sem.at[kv, span],
            device_id=device,
            device_id_type=MESH,
        )

    def send(span, device):
        if COMM:
            unit(core, span, device).start()

    def arrived(kv, span):
        if COMM:
            unit(kv, span, to_core).wait_recv()

    def place(x, distance):
        return x * RING + lax.rem(z + distance + RING, RING)

    def span_of(slot, side):
        return 2 * slot + (y_lo if side == 0 else 1 - y_lo)

    def relay(x, distance, side, *devices):
        span = span_of(place(x, distance), side)
        arrived(core, span)
        for device in devices:
            send(span, device)
        send(span, to_core)

    def z_even(e):
        for way in (1, -1):
            for side in (0, 1):
                devices = []
                if e < 3:
                    devices.append(along(2 * way))
                if e == 3 and side == 0 and way == 1:
                    devices.append(along(2))
                if side == 0:
                    devices.append(along(way))
                if side == 0 or e < 3:
                    devices.append(to_x)
                relay(x_lo, -way * 2 * e, side, *devices)

    def z_leaf(e):
        for way in (1, -1):
            relay(x_lo, -way * (2 * e - 1), 0, to_y, to_x)

    def z_part(e):
        if e < 4:
            z_even(e)
        else:
            relay(x_lo, -8, 0, to_y, to_x)
        z_leaf(e)

    def y_own(e):
        for way in (1, -1):
            relay(x_lo, -way * (2 * e - 1), 1)
        if e == 4:
            relay(x_lo, -8, 1)

    def x_part(e):
        if e == 0:
            relay(other_x, 0, 0)
            relay(other_x, 0, 1)
            return
        if e == 4:
            relay(other_x, -8, 0, to_y)
        for way in (1, -1):
            relay(other_x, -way * (2 * e - 1), 0, to_y)
        if e < 4:
            for way in (1, -1):
                if e < 3:
                    relay(other_x, -way * 2 * e, 0)
                    relay(other_x, -way * 2 * e, 1)
                else:
                    relay(other_x, -way * 2 * e, 0, to_y)

    def y_other(e):
        if e == 4:
            relay(other_x, -8, 1)
        for way in (1, -1):
            relay(other_x, -way * (2 * e - 1), 1)
        if e == 3:
            for way in (1, -1):
                relay(other_x, -way * 2 * e, 1)

    def ready(slot):
        for side in (0, 1):
            arrived(1 - core, span_of(slot, side))

    def attend(slots, own_slot=False):
        if not COMPUTE:
            return
        spans = [2 * slot + j for slot in slots for j in (0, 1)]
        keys = jnp.concatenate(
            [jnp.concatenate([buf[0, s], ext[s]], axis=1) for s in spans], axis=0
        )
        values = jnp.concatenate([buf[1, s] for s in spans], axis=1)
        values = jnp.concatenate(
            [values, jnp.ones((ONES, values.shape[1]), jnp.bfloat16)], axis=0
        )
        scores = jnp.dot(keys, qx[...], preferred_element_type=jnp.float32)
        if own_slot:
            key_row = lax.broadcasted_iota(jnp.int32, scores.shape, 0)
            query_row = lax.broadcasted_iota(jnp.int32, scores.shape, 1) % (2 * SPAN)
            later = (key_row > query_row) & ((key_row >= SPAN) == (query_row >= SPAN))
            scores = jnp.where(later, -BIG, scores)
        scores = scores * FACTOR
        highest = jnp.max(scores, axis=0, keepdims=True)
        if own_slot:
            new_top = highest
        else:
            old_top = top[0:1, :]
            new_top = jnp.maximum(old_top, highest)
        weights = jnp.exp2(scores - new_top).astype(jnp.bfloat16)
        mixed = jnp.dot(values, weights, preferred_element_type=jnp.float32)
        if own_slot:
            acc[...] = mixed
        else:
            acc[...] = acc[...] * jnp.exp2(old_top - new_top) + mixed
        top[0:1, :] = new_top

    local[1].wait()
    for j in (0, 1):
        block = vtmp[j * SPAN:(j + 1) * SPAN, :].astype(jnp.float32)
        buf[1, own + j] = block.T.astype(jnp.bfloat16)
    local[0].wait()
    if COMM:
        pl.semaphore_wait(barrier, 7)
    mine = [span_of(ctx, side) for side in (0, 1)]
    for device in (along(2), along(-2)):
        send(mine[0], device)
    for device in (along(2), along(-2)):
        send(mine[1], device)
    for device in (along(1), along(-1), to_x):
        send(mine[0], device)
    send(mine[1], to_x)

    def borders(lane):
        opens = jnp.where(lane < SPANS, lane * SPAN, 1 << 20)
        closes = jnp.where(lane < SPANS, lane * SPAN + SPAN, 1 << 20)
        end = jnp.int32(0)
        for d in range(DOCS):
            opens = jnp.where(lane == SPANS + d, end, opens)
            end = end + lens_ref[d]
            closes = jnp.where(lane == SPANS + d, end if d < DOCS - 1 else 1 << 20, closes)
        return opens, closes

    lane = lax.broadcasted_iota(jnp.int32, (1, DH), 1)
    opens, closes = borders(lane)
    row = lax.broadcasted_iota(jnp.int32, (DH, 1), 0)
    row_opens, row_closes = borders(row)

    def marks(s, carry):
        position = order_ref[s] * SPAN + lax.broadcasted_iota(jnp.int32, (SPAN, 1), 0)
        inside = (position >= opens) & (position < closes)
        ext[s] = jnp.where(inside, 1.0, 0.0).astype(jnp.bfloat16)
        return carry

    empty = jnp.where(lane == SPANS + DOCS, 1.0, 0.0) + jnp.zeros((SPAN, 1), jnp.float32)
    for j in (0, 1):
        ext[SPANS + j] = empty.astype(jnp.bfloat16)
        buf[0, SPANS + j] = jnp.zeros((SPAN, DH), jnp.bfloat16)
        buf[1, SPANS + j] = jnp.zeros((SPAN, DH), jnp.bfloat16)
        position = order_ref[own + j] * SPAN + lax.broadcasted_iota(jnp.int32, (1, SPAN), 1)
        outside = jnp.where((position >= row_opens) & (position < row_closes), 0.0, -BIG)
        after = jnp.where(row > order_ref[own + j], -BIG, 0.0) + jnp.zeros((1, SPAN), jnp.float32)
        last = jnp.where(row == SPANS + DOCS, -BIG, 0.0) + jnp.zeros((1, SPAN), jnp.float32)
        side_q = jnp.where(row < SPANS, after, jnp.where(row < SPANS + DOCS, outside, last))
        for h in range(4):
            qx[DH:, (2 * h + j) * SPAN:(2 * h + j + 1) * SPAN] = side_q.astype(jnp.bfloat16)
    lax.fori_loop(0, SPANS, marks, 0, unroll=4)
    local[2].wait()
    for h in range(4):
        qx[:DH, 2 * h * SPAN:2 * (h + 1) * SPAN] = (
            qtmp[h].astype(jnp.float32).T.astype(jnp.bfloat16)
        )

    attend([ctx], own_slot=True)
    x_part(0)
    z_part(1)

    parts = {
        1: [(y_own, 1), (z_part, 2), (x_part, 1)],
        2: [(y_other, 1), (y_own, 2), (z_part, 3)],
        3: [(x_part, 2)],
        4: [(z_part, 4), (y_own, 3), (y_other, 2)],
        5: [(x_part, 3)],
        6: [(y_own, 4), (x_part, 4), (y_other, 3)],
        7: [(y_other, 4)],
        8: [],
    }

    def turn(i, carry):
        for k, steps in parts.items():
            if steps:
                @pl.when(i == k)
                def _():
                    for step, e in steps:
                        step(e)

        far = 1 - lax.rem(i, 2)
        e = (i + 1) // 2
        last = e // 4
        x = x_lo * (1 - far) + other_x * far
        slots = [place(x, 1 - 2 * e), place(x, 2 * e - 1), place(x, -2 * e)]
        special = far * (SPANS // 2) + (1 - far) * (other_x * RING + z)
        slots.append(place(x, 2 * e) * (1 - last) + special * last)
        for slot in slots[:3]:
            ready(slot)

        @pl.when(i < 8)
        def _():
            ready(slots[3])

        attend(slots)
        return carry

    lax.fori_loop(1, 9, turn, 0)

    if COMPUTE:
        result = acc[:DH, :] / acc[DH:DH + 1, :]
        for h in range(4):
            out_ref[h] = result[:, 2 * h * SPAN:2 * (h + 1) * SPAN].T.astype(jnp.bfloat16)
    else:
        for h in range(4):
            out_ref[h] = (buf[0, 2 * h].astype(jnp.float32) + buf[1, 2 * h + 9]).astype(jnp.bfloat16)[:1, :] + jnp.zeros((256, DH), jnp.bfloat16)
    if COMM:
        pltpu.make_async_copy(buf.at[:, pl.ds(0, 62)], buf.at[:, pl.ds(0, 62)], send_sem).wait()


def body(queries, key_heads, value_heads, doc_lengths, span_order):
    heads, rows, _ = queries.shape
    shape = (key_heads.shape[0], 2, SPAN, DH)
    return pl.pallas_call(
        kernel,
        out_shape=jax.ShapeDtypeStruct(queries.shape, jnp.bfloat16),
        in_specs=[
            pl.BlockSpec(memory_space=pl.ANY),
            pl.BlockSpec(memory_space=pl.ANY),
            pl.BlockSpec(memory_space=pl.ANY),
            pl.BlockSpec(memory_space=pltpu.SMEM),
            pl.BlockSpec(memory_space=pltpu.SMEM),
        ],
        out_specs=pl.BlockSpec(memory_space=pltpu.VMEM),
        scratch_shapes=[
            pltpu.VMEM((2, SPANS + 2, SPAN, DH), jnp.bfloat16),
            pltpu.VMEM((SPANS + 2, SPAN, DH), jnp.bfloat16),
            pltpu.VMEM((2 * DH, heads * rows), jnp.bfloat16),
            pltpu.VMEM((heads, rows, DH), jnp.bfloat16),
            pltpu.VMEM((rows, DH), jnp.bfloat16),
            pltpu.VMEM((DH + ONES, heads * rows), jnp.float32),
            pltpu.VMEM((8, heads * rows), jnp.float32),
            pltpu.SemaphoreType.DMA,
            pltpu.SemaphoreType.DMA((2, SPANS)),
            pltpu.SemaphoreType.DMA((3,)),
        ],
        compiler_params=pltpu.CompilerParams(
            collective_id=0 if COMM else None, has_side_effects=True, vmem_limit_bytes=62 * 2**20
        ),
        cost_estimate=pl.CostEstimate(
            flops=4 * heads * rows * SPANS * SPAN * DH,
            bytes_accessed=2**20,
            transcendentals=heads * rows * SPANS * SPAN,
        ),
    )(queries, key_heads.reshape(shape), value_heads, doc_lengths, span_order)


def solution(mesh):
    return jax.shard_map(
        body,
        mesh=mesh,
        in_specs=(P("head", "ctx", None), P(None, "ctx", None), P(None, "ctx", None), P(), P()),
        out_specs=P("head", "ctx", None),
        check_vma=False,
    )
```

```python
import math

import jax
import jax.numpy as jnp
from jax import lax
from jax.experimental import pallas as pl
from jax.experimental.pallas import tpu as pltpu
from jax.sharding import PartitionSpec as P

MESH = pl.DeviceIdType.MESH
SPAN = 128
DH = 128
DOCS = 16
SPANS = 64
RING = 16
BIG = 131072.0
FACTOR = math.log2(math.e) / math.sqrt(DH)
ONES = 16
COMM = True
COMPUTE = True


PAIRS = [
    (("A", 1), ("A", -1)), (("A", 3), ("A", -3)),
    (("A", 2), ("A", -2)), (("B", 1), ("B", -1)),
    (("B", 3), ("B", -3)), (("A", 6), ("A", -6)),
    (("B", 2), ("B", -2)), (("A", 5), ("A", -5)),
    (("A", 4), ("A", -4)), (("A", 8), ("B", 0)),
    (("B", 6), ("B", -6)), (("A", 7), ("A", -7)),
    (("B", 5), ("B", -5)), (("B", 8), None),
    (("B", 4), ("B", -4)), (("B", 7), ("B", -7)),
]
PLACE = {}
for _n, _pair in enumerate(PAIRS):
    for _m, _slot in enumerate(_pair):
        for _side in (0, 1):
            PLACE[_slot, _side] = 4 * _n + 2 * _side + _m
PLACE[("A", 0), 0] = 64
PLACE[("A", 0), 1] = 65
OVER_X = (1, 4, 5, 6)
ORDER = [
    [("B", 0, 0), ("B", 0, 1), ("A", 3, 0), ("A", 2, 0), ("A", 1, 0), ("A", 1, 1),
     ("A", 3, 1), ("B", 3, 0), ("A", 6, 0)],
    [("A", 2, 1), ("B", 2, 0), ("A", 5, 0), ("A", 4, 0), ("B", 1, 0), ("B", 1, 1),
     ("B", 3, 1), ("A", 8, 0), ("A", 7, 0)],
    [("B", 6, 0), ("A", 6, 1), ("B", 5, 0)],
    [("B", 2, 1), ("B", 4, 0), ("A", 5, 1), ("B", 8, 0)],
    [("A", 4, 1), ("B", 7, 0), ("A", 8, 1)],
    [("B", 6, 1), ("A", 7, 1), ("B", 8, 1), ("B", 5, 1)],
    [("B", 4, 1), ("B", 7, 1)],
    [],
]
ALONG = {0: (3, 2, 1), 3: (6, 5, 4)}


def kernel(q_ref, k_ref, v_ref, lens_ref, order_ref, out_ref,
           buf, ext, qx, qtmp, vtmp, acc, top, send_sem, recv_sem, core_sem, local_sem):
    head = lax.axis_index("head")
    ctx = lax.axis_index("ctx")
    core = lax.rem(head, 2)
    y_lo = lax.rem(head // 2, 2)
    x_lo = ctx // RING
    z = lax.rem(ctx, RING)
    group = head // 4
    own = 2 * ctx
    other_x = 1 - x_lo

    local = [
        pltpu.make_async_copy(v_ref.at[group], vtmp, local_sem.at[0]),
        pltpu.make_async_copy(k_ref.at[group, y_lo], buf.at[0, 64], local_sem.at[1]),
        pltpu.make_async_copy(k_ref.at[group, 1 - y_lo], buf.at[0, 65], local_sem.at[2]),
        pltpu.make_async_copy(q_ref, qtmp, local_sem.at[3]),
    ]
    for copy in local:
        copy.start()

    empty_places = (PLACE[None, 0], PLACE[None, 1])
    for p in empty_places:
        buf[0, p] = jnp.zeros((SPAN, DH), jnp.bfloat16)
        buf[1, p] = jnp.zeros((SPAN, DH), jnp.bfloat16)

    def along(distance):
        return {"ctx": x_lo * RING + lax.rem(z + distance + RING, RING)}

    to_x = {"ctx": other_x * RING + z}
    to_y = {"head": head + 2 - 4 * y_lo}
    to_core = {"head": head + 1 - 2 * core}

    if COMM:
        barrier = pltpu.get_barrier_semaphore()
        for device in [along(d) for d in (1, -1, 2, -2, 3, -3)] + [to_x, to_y, to_core]:
            pl.semaphore_signal(barrier, inc=1, device_id=device, device_id_type=MESH)

    def unit(source, target, device):
        return pltpu.make_async_remote_copy(
            src_ref=buf.at[core, source],
            dst_ref=buf.at[core, target],
            send_sem=send_sem,
            recv_sem=recv_sem.at[target],
            device_id=device,
            device_id_type=MESH,
        )

    def pair(kv, n):
        return pltpu.make_async_remote_copy(
            src_ref=buf.at[kv, pl.ds(4 * n, 4)],
            dst_ref=buf.at[kv, pl.ds(4 * n, 4)],
            send_sem=send_sem,
            recv_sem=core_sem.at[n],
            device_id=to_core,
            device_id_type=MESH,
        )

    def send(source, target, device):
        if COMM:
            unit(source, target, device).start()

    def ways(distance):
        return (1,) if distance in (0, 8) else (1, -1)

    missing = [sum(slot is not None for slot in p) * 2 for p in PAIRS]

    def relay(kind, distance, side):
        signed = [-way * distance if distance not in (0, 8) else distance for way in ways(distance)]
        here = [PLACE[(kind, r), side] for r in signed]
        for p in here:
            if COMM:
                unit(p, p, to_core).wait_recv()
        if kind == "A":
            if distance == 6 and side == 0:
                up, down = PLACE[("A", -6), 0], PLACE[("A", 6), 0]
                send(up + core * (down - up), PLACE[("A", 8), 0], along(2 - 4 * core))
                for way in (1, -1):
                    send(PLACE[("A", -6 * way), 0], PLACE[("A", -7 * way), 0], along(way))
            if side == 0:
                for far in ALONG.get(distance, ()):
                    for way in (1, -1):
                        send(PLACE[("A", -way * distance), 0], PLACE[("A", -way * far), 0],
                             along(way * (far - distance)))
                if distance != 1:
                    for r, p in zip(signed, here):
                        send(p, PLACE[("A", r), 1], to_y)
            if side == 0 or distance in OVER_X:
                for r, p in zip(signed, here):
                    send(p, PLACE[("B", r), side], to_x)
        elif side == 0 and distance and distance not in OVER_X:
            for r, p in zip(signed, here):
                send(p, PLACE[("B", r), 1], to_y)
        for r in signed:
            n = [k for k, p in enumerate(PAIRS) if (kind, r) in p][0]
            missing[n] -= 1
            if missing[n] == 0 and COMM:
                pair(core, n).start()

    def attend(keys, values, own_slot=False):
        if not COMPUTE:
            return
        values = jnp.concatenate(
            [values, jnp.ones((ONES, values.shape[1]), jnp.bfloat16)], axis=0
        )
        scores = jnp.dot(keys, qx[...], preferred_element_type=jnp.float32)
        if own_slot:
            key_row = lax.broadcasted_iota(jnp.int32, scores.shape, 0)
            query_row = lax.broadcasted_iota(jnp.int32, scores.shape, 1) % (2 * SPAN)
            later = (key_row > query_row) & ((key_row >= SPAN) == (query_row >= SPAN))
            scores = jnp.where(later, -BIG, scores)
        scores = scores * FACTOR
        highest = jnp.max(scores, axis=0, keepdims=True)
        if own_slot:
            new_top = highest
        else:
            old_top = top[0:1, :]
            new_top = jnp.maximum(old_top, highest)
        weights = jnp.exp2(scores - new_top).astype(jnp.bfloat16)
        mixed = jnp.dot(values, weights, preferred_element_type=jnp.float32)
        if own_slot:
            acc[...] = mixed
        else:
            acc[...] = acc[...] * jnp.exp2(old_top - new_top) + mixed
        top[0:1, :] = new_top

    local[0].wait()
    for j in (0, 1):
        block = vtmp[j].astype(jnp.float32)
        buf[1, 64 + (y_lo if j == 0 else 1 - y_lo)] = block.T.astype(jnp.bfloat16)
    local[1].wait()
    local[2].wait()
    if COMM:
        pl.semaphore_wait(barrier, 9)
    for distance in ALONG[0]:
        for way in (1, -1):
            send(64, PLACE[("A", -way * distance), 0], along(way * distance))
    for side in (0, 1):
        send(64 + side, PLACE[("B", 0), side], to_x)
    for way in (1, -1):
        send(65, PLACE[("A", -way), 1], along(way))

    def borders(lane):
        opens = jnp.where(lane < SPANS, lane * SPAN, 1 << 20)
        closes = jnp.where(lane < SPANS, lane * SPAN + SPAN, 1 << 20)
        end = jnp.int32(0)
        for d in range(DOCS):
            opens = jnp.where(lane == SPANS + d, end, opens)
            end = end + lens_ref[d]
            closes = jnp.where(lane == SPANS + d, end if d < DOCS - 1 else 1 << 20, closes)
        return opens, closes

    lane = lax.broadcasted_iota(jnp.int32, (1, DH), 1)
    opens, closes = borders(lane)
    row = lax.broadcasted_iota(jnp.int32, (DH, 1), 0)
    row_opens, row_closes = borders(row)
    in_span = lax.broadcasted_iota(jnp.int32, (SPAN, 1), 0)

    for (slot, side), p in PLACE.items():
        if slot is None:
            marks = jnp.where(lane == SPANS + DOCS, 1.0, 0.0) + jnp.zeros((SPAN, 1), jnp.float32)
        else:
            kind, r = slot
            first = 2 * ((x_lo if kind == "A" else other_x) * RING + lax.rem(z + r + RING, RING))
            position = order_ref[first + (y_lo if side == 0 else 1 - y_lo)] * SPAN + in_span
            marks = jnp.where((position >= opens) & (position < closes), 1.0, 0.0)
        ext[p] = marks.astype(jnp.bfloat16)

    for j in (0, 1):
        position = order_ref[own + j] * SPAN + lax.broadcasted_iota(jnp.int32, (1, SPAN), 1)
        outside = jnp.where((position >= row_opens) & (position < row_closes), 0.0, -BIG)
        after = jnp.where(row > order_ref[own + j], -BIG, 0.0) + jnp.zeros((1, SPAN), jnp.float32)
        last = jnp.where(row == SPANS + DOCS, -BIG, 0.0) + jnp.zeros((1, SPAN), jnp.float32)
        side_q = jnp.where(row < SPANS, after, jnp.where(row < SPANS + DOCS, outside, last))
        for h in range(4):
            qx[DH:, (2 * h + j) * SPAN:(2 * h + j + 1) * SPAN] = side_q.astype(jnp.bfloat16)
    local[3].wait()
    for h in range(4):
        qx[:DH, 2 * h * SPAN:2 * (h + 1) * SPAN] = (
            qtmp[h].astype(jnp.float32).T.astype(jnp.bfloat16)
        )

    natural = [64 + y_lo, 65 - y_lo]
    attend(
        jnp.concatenate([jnp.concatenate([buf[0, p], ext[p]], axis=1) for p in natural], axis=0),
        jnp.concatenate([buf[1, p] for p in natural], axis=1),
        own_slot=True,
    )

    def turn(i, carry):
        for k, events in enumerate(ORDER):
            if events:
                @pl.when(i == k)
                def _():
                    for kind, distance, side in events:
                        relay(kind, distance, side)

        if COMM:
            pair(1 - core, 2 * i).wait_recv()
            pair(1 - core, 2 * i + 1).wait_recv()
        eight = pl.ds(8 * i, 8)
        attend(
            jnp.concatenate(
                [buf[0, eight].reshape(8 * SPAN, DH), ext[eight].reshape(8 * SPAN, DH)], axis=1
            ),
            jnp.concatenate([buf[1, 8 * i + j] for j in range(8)], axis=1),
        )
        return carry

    lax.fori_loop(0, len(ORDER), turn, 0)

    if COMPUTE:
        result = acc[:DH, :] / acc[DH:DH + 1, :]
        for h in range(4):
            out_ref[h] = result[:, 2 * h * SPAN:2 * (h + 1) * SPAN].T.astype(jnp.bfloat16)
    else:
        for h in range(4):
            out_ref[h] = (buf[0, 2 * h].astype(jnp.float32) + buf[1, 2 * h + 9]).astype(jnp.bfloat16)[:1, :] + jnp.zeros((256, DH), jnp.bfloat16)
    if COMM:
        pltpu.make_async_copy(buf.at[:, pl.ds(0, 63)], buf.at[:, pl.ds(0, 63)], send_sem).wait()


def body(queries, key_heads, value_heads, doc_lengths, span_order):
    heads, rows, _ = queries.shape
    shape = (key_heads.shape[0], 2, SPAN, DH)
    return pl.pallas_call(
        kernel,
        out_shape=jax.ShapeDtypeStruct(queries.shape, jnp.bfloat16),
        in_specs=[
            pl.BlockSpec(memory_space=pl.ANY),
            pl.BlockSpec(memory_space=pl.ANY),
            pl.BlockSpec(memory_space=pl.ANY),
            pl.BlockSpec(memory_space=pltpu.SMEM),
            pl.BlockSpec(memory_space=pltpu.SMEM),
        ],
        out_specs=pl.BlockSpec(memory_space=pltpu.VMEM),
        scratch_shapes=[
            pltpu.VMEM((2, SPANS + 2, SPAN, DH), jnp.bfloat16),
            pltpu.VMEM((SPANS + 2, SPAN, DH), jnp.bfloat16),
            pltpu.VMEM((2 * DH, heads * rows), jnp.bfloat16),
            pltpu.VMEM((heads, rows, DH), jnp.bfloat16),
            pltpu.VMEM((2, SPAN, DH), jnp.bfloat16),
            pltpu.VMEM((DH + ONES, heads * rows), jnp.float32),
            pltpu.VMEM((8, heads * rows), jnp.float32),
            pltpu.SemaphoreType.DMA,
            pltpu.SemaphoreType.DMA((SPANS,)),
            pltpu.SemaphoreType.DMA((len(PAIRS),)),
            pltpu.SemaphoreType.DMA((4,)),
        ],
        compiler_params=pltpu.CompilerParams(
            collective_id=0 if COMM else None, has_side_effects=True, vmem_limit_bytes=62 * 2**20
        ),
        cost_estimate=pl.CostEstimate(
            flops=4 * heads * rows * SPANS * SPAN * DH,
            bytes_accessed=2**20,
            transcendentals=heads * rows * SPANS * SPAN,
        ),
    )(queries, key_heads.reshape(shape), value_heads.reshape(shape), doc_lengths, span_order)


def solution(mesh):
    return jax.shard_map(
        body,
        mesh=mesh,
        in_specs=(P("head", "ctx", None), P(None, "ctx", None), P(None, "ctx", None), P(), P()),
        out_specs=P("head", "ctx", None),
        check_vma=False,
    )
```

```python
import math

import jax
import jax.numpy as jnp
from jax import lax
from jax.experimental import pallas as pl
from jax.experimental.pallas import tpu as pltpu
from jax.sharding import PartitionSpec as P

MESH = pl.DeviceIdType.MESH
SPAN = 128
DH = 128
DOCS = 16
SPANS = 64
RING = 16
BIG = 131072.0
FACTOR = math.log2(math.e) / math.sqrt(DH)
ONES = 16


BLOCKS = [
    [("B", 0, 0), ("B", 0, 1), ("A", 3, 0), ("A", 2, 0), ("A", 1, 0)],
    [("A", 1, 1), ("A", 3, 1), ("B", 3, 0), ("A", 6, 0)],
    [("A", 2, 1), ("B", 2, 0), ("A", 5, 0), ("A", 4, 0)],
    [("B", 1, 0), ("B", 1, 1), ("B", 3, 1), ("A", 8, 0), None],
    [("A", 7, 0), ("B", 6, 0), ("A", 6, 1), ("B", 5, 0)],
    [("B", 2, 1), ("B", 4, 0), ("A", 5, 1), ("B", 8, 0), None],
    [("A", 4, 1), ("B", 7, 0), ("A", 8, 1), ("B", 6, 1), ("B", 8, 1)],
    [("A", 7, 1), ("B", 5, 1), ("B", 4, 1), ("B", 7, 1)],
]
ORDER = [
    [("B", 0, 0), ("B", 0, 1), ("A", 3, 0), ("A", 2, 0), ("A", 1, 0), ("A", 1, 1),
     ("A", 3, 1), ("B", 3, 0), ("A", 6, 0), ("A", 2, 1), ("B", 2, 0), ("A", 5, 0), ("A", 4, 0),
     ("B", 1, 0)],
    [("B", 1, 1), ("B", 3, 1), ("A", 8, 0), ("A", 7, 0)],
    [("B", 6, 0), ("A", 6, 1)],
    [("B", 5, 0), ("B", 2, 1), ("B", 4, 0), ("A", 5, 1), ("B", 8, 0)],
    [("A", 4, 1), ("B", 7, 0)],
    [("A", 8, 1), ("B", 6, 1), ("A", 7, 1), ("B", 8, 1)],
    [("B", 5, 1), ("B", 4, 1), ("B", 7, 1)],
    [],
]


def signed(distance):
    return (distance,) if distance in (0, 8) else (-distance, distance)


SPOTS = []
for _block in BLOCKS:
    for _batch in _block:
        if _batch is None:
            SPOTS.append(None)
        else:
            SPOTS.extend(((_batch[0], r), _batch[2]) for r in signed(_batch[1]))
SPOTS += [(("A", 0), 0), (("A", 0), 1)]
PLACE = {spot: p for p, spot in enumerate(SPOTS) if spot is not None}
EMPTY = [p for p, spot in enumerate(SPOTS) if spot is None]
LAST = [
    [e for events in ORDER for e in events
     if any(((e[0], r), e[2]) in SPOTS[n:n + 4] for r in signed(e[1]))][-1]
    for n in range(0, SPANS, 4)
]
OVER_X = (1, 4, 5, 6)
ALONG = {0: (3, 2, 1), 3: (6, 5, 4)}


def kernel(q_ref, k_ref, v_ref, lens_in, order_in, out_ref,
           lens_ref, order_ref, buf, ext, qx, qtmp, vtmp, acc, top, send_sem, recv_sem, core_sem, local_sem):
    head = lax.axis_index("head")
    ctx = lax.axis_index("ctx")
    core = lax.rem(head, 2)
    y_lo = lax.rem(head // 2, 2)
    x_lo = ctx // RING
    z = lax.rem(ctx, RING)
    group = head // 4
    own = 2 * ctx
    other_x = 1 - x_lo

    local = [
        pltpu.make_async_copy(v_ref.at[group], vtmp, local_sem.at[0]),
        pltpu.make_async_copy(k_ref.at[group, y_lo], buf.at[0, 64], local_sem.at[1]),
        pltpu.make_async_copy(k_ref.at[group, 1 - y_lo], buf.at[0, 65], local_sem.at[2]),
        pltpu.make_async_copy(lens_in, lens_ref, local_sem.at[4]),
        pltpu.make_async_copy(order_in, order_ref, local_sem.at[5]),
        pltpu.make_async_copy(q_ref, qtmp, local_sem.at[3]),
    ]
    for copy in local:
        copy.start()

    for p in EMPTY:
        buf[0, p] = jnp.zeros((SPAN, DH), jnp.bfloat16)
        buf[1, p] = jnp.zeros((SPAN, DH), jnp.bfloat16)

    def along(distance):
        return {"ctx": x_lo * RING + lax.rem(z + distance + RING, RING)}

    to_x = {"ctx": other_x * RING + z}
    to_y = {"head": head + 2 - 4 * y_lo}
    to_core = {"head": head + 1 - 2 * core}

    barrier = pltpu.get_barrier_semaphore()
    for device in [along(d) for d in (1, -1, 2, -2, 3, -3)] + [to_x, to_y, to_core]:
        pl.semaphore_signal(barrier, inc=1, device_id=device, device_id_type=MESH)

    def unit(source, target, device):
        return pltpu.make_async_remote_copy(
            src_ref=buf.at[core, source],
            dst_ref=buf.at[core, target],
            send_sem=send_sem,
            recv_sem=recv_sem.at[target],
            device_id=device,
            device_id_type=MESH,
        )

    def pair(kv, n):
        return pltpu.make_async_remote_copy(
            src_ref=buf.at[kv, pl.ds(4 * n, 4)],
            dst_ref=buf.at[kv, pl.ds(4 * n, 4)],
            send_sem=send_sem,
            recv_sem=core_sem.at[n],
            device_id=to_core,
            device_id_type=MESH,
        )

    def send(source, target, device):
        unit(source, target, device).start()

    def relay(kind, distance, side):
        rels = signed(distance)
        here = [PLACE[(kind, r), side] for r in rels]
        for p in here:
            unit(p, p, to_core).wait_recv()
        if kind == "A":
            if distance == 6 and side == 0:
                up, down = PLACE[("A", -6), 0], PLACE[("A", 6), 0]
                send(up + core * (down - up), PLACE[("A", 8), 0], along(2 - 4 * core))
                for way in (1, -1):
                    send(PLACE[("A", -6 * way), 0], PLACE[("A", -7 * way), 0], along(way))
            if side == 0:
                for far in ALONG.get(distance, ()):
                    for way in (1, -1):
                        send(PLACE[("A", -way * distance), 0], PLACE[("A", -way * far), 0],
                             along(way * (far - distance)))
                if distance != 1:
                    for r, p in zip(rels, here):
                        send(p, PLACE[("A", r), 1], to_y)
            if side == 0 or distance in OVER_X:
                for r, p in zip(rels, here):
                    send(p, PLACE[("B", r), side], to_x)
        elif side == 0 and distance and distance not in OVER_X:
            for r, p in zip(rels, here):
                send(p, PLACE[("B", r), 1], to_y)
        for n, event in enumerate(LAST):
            if event == (kind, distance, side):
                pair(core, n).start()

    def attend(keys, values, own_slot=False):
        values = jnp.concatenate(
            [values, jnp.ones((ONES, values.shape[1]), jnp.bfloat16)], axis=0
        )
        scores = jnp.dot(keys, qx[...], preferred_element_type=jnp.float32)
        if own_slot:
            key_row = lax.broadcasted_iota(jnp.int32, scores.shape, 0)
            query_row = lax.broadcasted_iota(jnp.int32, scores.shape, 1) % (2 * SPAN)
            later = (key_row > query_row) & ((key_row >= SPAN) == (query_row >= SPAN))
            scores = jnp.where(later, -BIG, scores)
        scores = scores * FACTOR
        highest = jnp.max(scores, axis=0, keepdims=True)
        if own_slot:
            new_top = highest
        else:
            old_top = top[0:1, :]
            new_top = jnp.maximum(old_top, highest)
        weights = jnp.exp2(scores - new_top).astype(jnp.bfloat16)
        mixed = jnp.dot(values, weights, preferred_element_type=jnp.float32)
        if own_slot:
            acc[...] = mixed
        else:
            acc[...] = acc[...] * jnp.exp2(old_top - new_top) + mixed
        top[0:1, :] = new_top

    local[0].wait()
    for j in (0, 1):
        block = vtmp[j].astype(jnp.float32)
        buf[1, 64 + (y_lo if j == 0 else 1 - y_lo)] = block.T.astype(jnp.bfloat16)
    local[1].wait()
    local[2].wait()
    pl.semaphore_wait(barrier, 9)
    for distance in ALONG[0]:
        for way in (1, -1):
            send(64, PLACE[("A", -way * distance), 0], along(way * distance))
    for side in (0, 1):
        send(64 + side, PLACE[("B", 0), side], to_x)
    for way in (1, -1):
        send(65, PLACE[("A", -way), 1], along(way))

    local[3].wait()
    local[4].wait()

    def borders(lane):
        opens = jnp.where(lane < SPANS, lane * SPAN, 1 << 20)
        closes = jnp.where(lane < SPANS, lane * SPAN + SPAN, 1 << 20)
        end = jnp.int32(0)
        for d in range(DOCS):
            opens = jnp.where(lane == SPANS + d, end, opens)
            end = end + lens_ref[d]
            closes = jnp.where(lane == SPANS + d, end if d < DOCS - 1 else 1 << 20, closes)
        return opens, closes

    lane = lax.broadcasted_iota(jnp.int32, (1, DH), 1)
    opens, closes = borders(lane)
    row = lax.broadcasted_iota(jnp.int32, (DH, 1), 0)
    row_opens, row_closes = borders(row)
    in_span = lax.broadcasted_iota(jnp.int32, (SPAN, 1), 0)

    for p, spot in enumerate(SPOTS):
        if spot is None:
            marks = jnp.where(lane == SPANS + DOCS, 1.0, 0.0) + jnp.zeros((SPAN, 1), jnp.float32)
        else:
            (kind, r), side = spot
            first = 2 * ((x_lo if kind == "A" else other_x) * RING + lax.rem(z + r + RING, RING))
            position = order_ref[first + (y_lo if side == 0 else 1 - y_lo)] * SPAN + in_span
            marks = jnp.where((position >= opens) & (position < closes), 1.0, 0.0)
        ext[p] = marks.astype(jnp.bfloat16)

    for j in (0, 1):
        position = order_ref[own + j] * SPAN + lax.broadcasted_iota(jnp.int32, (1, SPAN), 1)
        outside = jnp.where((position >= row_opens) & (position < row_closes), 0.0, -BIG)
        after = jnp.where(row > order_ref[own + j], -BIG, 0.0) + jnp.zeros((1, SPAN), jnp.float32)
        last = jnp.where(row == SPANS + DOCS, -BIG, 0.0) + jnp.zeros((1, SPAN), jnp.float32)
        side_q = jnp.where(row < SPANS, after, jnp.where(row < SPANS + DOCS, outside, last))
        for h in range(4):
            qx[DH:, (2 * h + j) * SPAN:(2 * h + j + 1) * SPAN] = side_q.astype(jnp.bfloat16)
    local[5].wait()
    for h in range(4):
        qx[:DH, 2 * h * SPAN:2 * (h + 1) * SPAN] = (
            qtmp[h].astype(jnp.float32).T.astype(jnp.bfloat16)
        )

    natural = [64 + y_lo, 65 - y_lo]
    attend(
        jnp.concatenate([jnp.concatenate([buf[0, p], ext[p]], axis=1) for p in natural], axis=0),
        jnp.concatenate([buf[1, p] for p in natural], axis=1),
        own_slot=True,
    )

    def turn(i, carry):
        for k, events in enumerate(ORDER):
            if events:
                @pl.when(i == k)
                def _():
                    for kind, distance, side in events:
                        relay(kind, distance, side)

        pair(1 - core, 2 * i).wait_recv()
        pair(1 - core, 2 * i + 1).wait_recv()
        eight = pl.ds(8 * i, 8)
        attend(
            jnp.concatenate(
                [buf[0, eight].reshape(8 * SPAN, DH), ext[eight].reshape(8 * SPAN, DH)], axis=1
            ),
            jnp.concatenate([buf[1, 8 * i + j] for j in range(8)], axis=1),
        )
        return carry

    lax.fori_loop(0, len(ORDER), turn, 0)

    result = acc[:DH, :] / acc[DH:DH + 1, :]
    for h in range(4):
        out_ref[h] = result[:, 2 * h * SPAN:2 * (h + 1) * SPAN].T.astype(jnp.bfloat16)
    pltpu.make_async_copy(buf.at[:, pl.ds(0, 63)], buf.at[:, pl.ds(0, 63)], send_sem).wait()


def body(queries, key_heads, value_heads, doc_lengths, span_order):
    heads, rows, _ = queries.shape
    shape = (key_heads.shape[0], 2, SPAN, DH)
    return pl.pallas_call(
        kernel,
        out_shape=jax.ShapeDtypeStruct(queries.shape, jnp.bfloat16),
        in_specs=[
            pl.BlockSpec(memory_space=pl.ANY),
            pl.BlockSpec(memory_space=pl.ANY),
            pl.BlockSpec(memory_space=pl.ANY),
            pl.BlockSpec(memory_space=pl.ANY),
            pl.BlockSpec(memory_space=pl.ANY),
        ],
        out_specs=pl.BlockSpec(memory_space=pltpu.VMEM),
        scratch_shapes=[
            pltpu.SMEM((DOCS,), jnp.int32),
            pltpu.SMEM((SPANS,), jnp.int32),
            pltpu.VMEM((2, SPANS + 2, SPAN, DH), jnp.bfloat16),
            pltpu.VMEM((SPANS + 2, SPAN, DH), jnp.bfloat16),
            pltpu.VMEM((2 * DH, heads * rows), jnp.bfloat16),
            pltpu.VMEM((heads, rows, DH), jnp.bfloat16),
            pltpu.VMEM((2, SPAN, DH), jnp.bfloat16),
            pltpu.VMEM((DH + ONES, heads * rows), jnp.float32),
            pltpu.VMEM((8, heads * rows), jnp.float32),
            pltpu.SemaphoreType.DMA,
            pltpu.SemaphoreType.DMA((SPANS,)),
            pltpu.SemaphoreType.DMA((SPANS // 4,)),
            pltpu.SemaphoreType.DMA((6,)),
        ],
        compiler_params=pltpu.CompilerParams(
            collective_id=0, has_side_effects=True, vmem_limit_bytes=62 * 2**20
        ),
        cost_estimate=pl.CostEstimate(
            flops=4 * heads * rows * SPANS * SPAN * DH,
            bytes_accessed=2**20,
            transcendentals=heads * rows * SPANS * SPAN,
        ),
    )(queries, key_heads.reshape(shape), value_heads.reshape(shape), doc_lengths, span_order)


def solution(mesh):
    return jax.shard_map(
        body,
        mesh=mesh,
        in_specs=(P("head", "ctx", None), P(None, "ctx", None), P(None, "ctx", None), P(), P()),
        out_specs=P("head", "ctx", None),
        check_vma=False,
    )
```

```python
import math

import jax
import jax.numpy as jnp
from jax import lax
from jax.experimental import pallas as pl
from jax.experimental.pallas import tpu as pltpu
from jax.sharding import PartitionSpec as P

MESH = pl.DeviceIdType.MESH
SPAN = 128
DH = 128
DOCS = 16
SPANS = 64
RING = 16
BIG = 131072.0
FACTOR = math.log2(math.e) / math.sqrt(DH)
ONES = 16


BLOCKS = [
    [("B", 0, 0), ("B", 0, 1), ("A", 3, 0), ("A", 2, 0), ("A", 1, 0)],
    [("A", 1, 1), ("A", 3, 1), ("B", 3, 0), ("A", 6, 0)],
    [("A", 2, 1), ("B", 2, 0), ("A", 5, 0), ("A", 4, 0)],
    [("B", 1, 0), ("B", 1, 1), ("B", 3, 1), ("A", 8, 0), None],
    [("A", 7, 0), ("B", 6, 0), ("A", 6, 1), ("B", 5, 0)],
    [("B", 2, 1), ("B", 4, 0), ("A", 5, 1), ("B", 8, 0), None],
    [("A", 4, 1), ("B", 7, 0), ("A", 8, 1), ("B", 6, 1), ("B", 8, 1)],
    [("A", 7, 1), ("B", 5, 1), ("B", 4, 1), ("B", 7, 1)],
]
ORDER = [
    [("B", 0, 0), ("B", 0, 1), ("A", 3, 0), ("A", 2, 0), ("A", 1, 0), ("A", 1, 1),
     ("A", 3, 1), ("B", 3, 0), ("A", 6, 0), ("A", 2, 1), ("B", 2, 0), ("A", 5, 0), ("A", 4, 0),
     ("B", 1, 0)],
    [("B", 1, 1), ("B", 3, 1), ("A", 8, 0), ("A", 7, 0)],
    [("B", 6, 0), ("A", 6, 1)],
    [("B", 5, 0), ("B", 2, 1), ("B", 4, 0), ("A", 5, 1), ("B", 8, 0)],
    [("A", 4, 1), ("B", 7, 0)],
    [("A", 8, 1), ("B", 6, 1), ("A", 7, 1), ("B", 8, 1)],
    [("B", 5, 1), ("B", 4, 1), ("B", 7, 1)],
    [],
]


def signed(distance):
    return (distance,) if distance in (0, 8) else (-distance, distance)


SPOTS = []
for _block in BLOCKS:
    for _batch in _block:
        if _batch is None:
            SPOTS.append(None)
        else:
            SPOTS.extend(((_batch[0], r), _batch[2]) for r in signed(_batch[1]))
SPOTS += [(("A", 0), 0), (("A", 0), 1)]
PLACE = {spot: p for p, spot in enumerate(SPOTS) if spot is not None}
EMPTY = [p for p, spot in enumerate(SPOTS) if spot is None]
LAST = [
    [e for events in ORDER for e in events
     if any(((e[0], r), e[2]) in SPOTS[n:n + 4] for r in signed(e[1]))][-1]
    for n in range(0, SPANS, 4)
]
OVER_X = (1, 4, 5, 6)
ALONG = {0: (3, 2, 1), 3: (6, 5, 4)}


def kernel(q_ref, k_ref, v_ref, lens_in, order_in, out_ref,
           lens_ref, order_ref, buf, ext, qx, qtmp, vtmp, acc, top, send_sem, recv_sem, core_sem, local_sem):
    head = lax.axis_index("head")
    ctx = lax.axis_index("ctx")
    core = lax.rem(head, 2)
    y_lo = lax.rem(head // 2, 2)
    x_lo = ctx // RING
    z = lax.rem(ctx, RING)
    group = head // 4
    own = 2 * ctx
    other_x = 1 - x_lo

    local = [
        pltpu.make_async_copy(v_ref.at[group], vtmp, local_sem.at[0]),
        pltpu.make_async_copy(k_ref.at[group, y_lo], buf.at[0, 64], local_sem.at[1]),
        pltpu.make_async_copy(k_ref.at[group, 1 - y_lo], buf.at[0, 65], local_sem.at[2]),
        pltpu.make_async_copy(lens_in, lens_ref, local_sem.at[4]),
        pltpu.make_async_copy(order_in, order_ref, local_sem.at[5]),
        pltpu.make_async_copy(q_ref, qtmp, local_sem.at[3]),
    ]
    for copy in local:
        copy.start()

    for p in EMPTY:
        buf[0, p] = jnp.zeros((SPAN, DH), jnp.bfloat16)
        buf[1, p] = jnp.zeros((SPAN, DH), jnp.bfloat16)

    def along(distance):
        return {"ctx": x_lo * RING + lax.rem(z + distance + RING, RING)}

    to_x = {"ctx": other_x * RING + z}
    to_y = {"head": head + 2 - 4 * y_lo}
    to_core = {"head": head + 1 - 2 * core}

    barrier = pltpu.get_barrier_semaphore()
    for device in [along(d) for d in (1, -1, 2, -2, 3, -3)] + [to_x, to_y, to_core]:
        pl.semaphore_signal(barrier, inc=1, device_id=device, device_id_type=MESH)

    def unit(source, target, device):
        return pltpu.make_async_remote_copy(
            src_ref=buf.at[core, source],
            dst_ref=buf.at[core, target],
            send_sem=send_sem,
            recv_sem=recv_sem.at[target],
            device_id=device,
            device_id_type=MESH,
        )

    def pair(kv, n):
        return pltpu.make_async_remote_copy(
            src_ref=buf.at[kv, pl.ds(4 * n, 4)],
            dst_ref=buf.at[kv, pl.ds(4 * n, 4)],
            send_sem=send_sem,
            recv_sem=core_sem.at[n],
            device_id=to_core,
            device_id_type=MESH,
        )

    def send(source, target, device):
        unit(source, target, device).start()

    def relay(kind, distance, side):
        rels = signed(distance)
        here = [PLACE[(kind, r), side] for r in rels]
        for p in here:
            unit(p, p, to_core).wait_recv()
        if kind == "A":
            if distance == 6 and side == 0:
                up, down = PLACE[("A", -6), 0], PLACE[("A", 6), 0]
                send(up + core * (down - up), PLACE[("A", 8), 0], along(2 - 4 * core))
                for way in (1, -1):
                    send(PLACE[("A", -6 * way), 0], PLACE[("A", -7 * way), 0], along(way))
            if side == 0:
                for far in ALONG.get(distance, ()):
                    for way in (1, -1):
                        send(PLACE[("A", -way * distance), 0], PLACE[("A", -way * far), 0],
                             along(way * (far - distance)))
                if distance != 1:
                    for r, p in zip(rels, here):
                        send(p, PLACE[("A", r), 1], to_y)
            if side == 0 or distance in OVER_X:
                for r, p in zip(rels, here):
                    send(p, PLACE[("B", r), side], to_x)
        elif side == 0 and distance and distance not in OVER_X:
            for r, p in zip(rels, here):
                send(p, PLACE[("B", r), 1], to_y)
        for n, event in enumerate(LAST):
            if event == (kind, distance, side):
                pair(core, n).start()

    def attend(keys, values, own_slot=False):
        values = jnp.concatenate(
            [values, jnp.ones((ONES, values.shape[1]), jnp.bfloat16)], axis=0
        )
        scores = jnp.dot(keys, qx[...], preferred_element_type=jnp.float32)
        if own_slot:
            key_row = lax.broadcasted_iota(jnp.int32, scores.shape, 0)
            query_row = lax.broadcasted_iota(jnp.int32, scores.shape, 1) % (2 * SPAN)
            later = (key_row > query_row) & ((key_row >= SPAN) == (query_row >= SPAN))
            scores = jnp.where(later, -BIG, scores)
        scores = scores * FACTOR
        highest = jnp.max(scores, axis=0, keepdims=True)
        if own_slot:
            new_top = highest
        else:
            old_top = top[0:1, :]
            new_top = jnp.maximum(old_top, highest)
        weights = jnp.exp2(scores - new_top).astype(jnp.bfloat16)
        mixed = jnp.dot(values, weights, preferred_element_type=jnp.float32)
        if own_slot:
            acc[...] = mixed
        else:
            acc[...] = acc[...] * jnp.exp2(old_top - new_top) + mixed
        top[0:1, :] = new_top

    local[0].wait()
    for j in (0, 1):
        block = vtmp[j].astype(jnp.float32)
        buf[1, 64 + (y_lo if j == 0 else 1 - y_lo)] = block.T.astype(jnp.bfloat16)
    local[1].wait()
    local[2].wait()
    pl.semaphore_wait(barrier, 9)
    for distance in ALONG[0]:
        for way in (1, -1):
            send(64, PLACE[("A", -way * distance), 0], along(way * distance))
    for side in (0, 1):
        send(64 + side, PLACE[("B", 0), side], to_x)
    for way in (1, -1):
        send(65, PLACE[("A", -way), 1], along(way))

    local[3].wait()
    local[4].wait()

    def borders(lane):
        opens = jnp.where(lane < SPANS, lane * SPAN, 1 << 20)
        closes = jnp.where(lane < SPANS, lane * SPAN + SPAN, 1 << 20)
        end = jnp.int32(0)
        for d in range(DOCS):
            opens = jnp.where(lane == SPANS + d, end, opens)
            end = end + lens_ref[d]
            closes = jnp.where(lane == SPANS + d, end if d < DOCS - 1 else 1 << 20, closes)
        return opens, closes

    lane = lax.broadcasted_iota(jnp.int32, (1, DH), 1)
    opens, closes = borders(lane)
    row = lax.broadcasted_iota(jnp.int32, (DH, 1), 0)
    row_opens, row_closes = borders(row)
    in_span = lax.broadcasted_iota(jnp.int32, (SPAN, 1), 0)

    for p, spot in enumerate(SPOTS):
        if spot is None:
            marks = jnp.where(lane == SPANS + DOCS, 1.0, 0.0) + jnp.zeros((SPAN, 1), jnp.float32)
        else:
            (kind, r), side = spot
            first = 2 * ((x_lo if kind == "A" else other_x) * RING + lax.rem(z + r + RING, RING))
            position = order_ref[first + (y_lo if side == 0 else 1 - y_lo)] * SPAN + in_span
            marks = jnp.where((position >= opens) & (position < closes), 1.0, 0.0)
        ext[p] = marks.astype(jnp.bfloat16)

    for j in (0, 1):
        position = order_ref[own + j] * SPAN + lax.broadcasted_iota(jnp.int32, (1, SPAN), 1)
        outside = jnp.where((position >= row_opens) & (position < row_closes), 0.0, -BIG)
        after = jnp.where(row > order_ref[own + j], -BIG, 0.0) + jnp.zeros((1, SPAN), jnp.float32)
        last = jnp.where(row == SPANS + DOCS, -BIG, 0.0) + jnp.zeros((1, SPAN), jnp.float32)
        side_q = jnp.where(row < SPANS, after, jnp.where(row < SPANS + DOCS, outside, last))
        for h in range(4):
            qx[DH:, (2 * h + j) * SPAN:(2 * h + j + 1) * SPAN] = side_q.astype(jnp.bfloat16)
    local[5].wait()
    for h in range(4):
        qx[:DH, 2 * h * SPAN:2 * (h + 1) * SPAN] = (
            qtmp[h].astype(jnp.float32).T.astype(jnp.bfloat16)
        )

    natural = [64 + y_lo, 65 - y_lo]
    attend(
        jnp.concatenate([jnp.concatenate([buf[0, p], ext[p]], axis=1) for p in natural], axis=0),
        jnp.concatenate([buf[1, p] for p in natural], axis=1),
        own_slot=True,
    )

    def turn(i, carry):
        for k, events in enumerate(ORDER):
            if events:
                @pl.when(i == k)
                def _():
                    for kind, distance, side in events:
                        relay(kind, distance, side)

        pair(1 - core, 2 * i).wait_recv()
        pair(1 - core, 2 * i + 1).wait_recv()
        eight = pl.ds(8 * i, 8)
        attend(
            jnp.concatenate(
                [buf[0, eight].reshape(8 * SPAN, DH), ext[eight].reshape(8 * SPAN, DH)], axis=1
            ),
            jnp.concatenate([buf[1, 8 * i + j] for j in range(8)], axis=1),
        )
        return carry

    lax.fori_loop(0, len(ORDER), turn, 0)

    result = acc[:DH, :] / acc[DH:DH + 1, :]
    for h in range(4):
        out_ref[h] = result[:, 2 * h * SPAN:2 * (h + 1) * SPAN].T.astype(jnp.bfloat16)
    pltpu.make_async_copy(buf.at[:, pl.ds(0, 63)], buf.at[:, pl.ds(0, 63)], send_sem).wait()


def body(queries, key_heads, value_heads, doc_lengths, span_order):
    heads, rows, _ = queries.shape
    shape = (key_heads.shape[0], 2, SPAN, DH)
    return pl.pallas_call(
        kernel,
        out_shape=jax.ShapeDtypeStruct(queries.shape, jnp.bfloat16),
        in_specs=[
            pl.BlockSpec(memory_space=pl.ANY),
            pl.BlockSpec(memory_space=pl.ANY),
            pl.BlockSpec(memory_space=pl.ANY),
            pl.BlockSpec(memory_space=pl.ANY),
            pl.BlockSpec(memory_space=pl.ANY),
        ],
        out_specs=pl.BlockSpec(memory_space=pltpu.VMEM),
        scratch_shapes=[
            pltpu.SMEM((DOCS,), jnp.int32),
            pltpu.SMEM((SPANS,), jnp.int32),
            pltpu.VMEM((2, SPANS + 2, SPAN, DH), jnp.bfloat16),
            pltpu.VMEM((SPANS + 2, SPAN, DH), jnp.bfloat16),
            pltpu.VMEM((2 * DH, heads * rows), jnp.bfloat16),
            pltpu.VMEM((heads, rows, DH), jnp.bfloat16),
            pltpu.VMEM((2, SPAN, DH), jnp.bfloat16),
            pltpu.VMEM((DH + ONES, heads * rows), jnp.float32),
            pltpu.VMEM((8, heads * rows), jnp.float32),
            pltpu.SemaphoreType.DMA,
            pltpu.SemaphoreType.DMA((SPANS,)),
            pltpu.SemaphoreType.DMA((SPANS // 4,)),
            pltpu.SemaphoreType.DMA((6,)),
        ],
        compiler_params=pltpu.CompilerParams(
            collective_id=0, has_side_effects=True, vmem_limit_bytes=54784 * 2**10
        ),
        cost_estimate=pl.CostEstimate(
            flops=4 * heads * rows * SPANS * SPAN * DH,
            bytes_accessed=2**20,
            transcendentals=heads * rows * SPANS * SPAN,
        ),
    )(queries, key_heads.reshape(shape), value_heads.reshape(shape), doc_lengths, span_order)


def solution(mesh):
    return jax.shard_map(
        body,
        mesh=mesh,
        in_specs=(P("head", "ctx", None), P(None, "ctx", None), P(None, "ctx", None), P(), P()),
        out_specs=P("head", "ctx", None),
        check_vma=False,
    )
```

```python
import math

import jax
import jax.numpy as jnp
from jax import lax
from jax.experimental import pallas as pl
from jax.experimental.pallas import tpu as pltpu
from jax.sharding import PartitionSpec as P

MESH = pl.DeviceIdType.MESH
SPAN = 128
DH = 128
DOCS = 16
SPANS = 64
RING = 16
BIG = 131072.0
FACTOR = math.log2(math.e) / math.sqrt(DH)
ONES = 16


BLOCKS = [
    [("B", 0, 0), ("B", 0, 1), ("A", 3, 0), ("A", 2, 0), ("A", 1, 0)],
    [("A", 1, 1), ("A", 3, 1), ("B", 3, 0), ("A", 6, 0)],
    [("A", 2, 1), ("B", 2, 0), ("A", 5, 0), ("A", 4, 0)],
    [("B", 1, 0), ("B", 1, 1), ("B", 3, 1), ("A", 8, 0), None],
    [("A", 7, 0), ("B", 6, 0), ("A", 6, 1), ("B", 5, 0)],
    [("B", 2, 1), ("B", 4, 0), ("A", 5, 1), ("B", 8, 0), None],
    [("A", 4, 1), ("B", 7, 0), ("A", 8, 1), ("B", 6, 1), ("B", 8, 1)],
    [("A", 7, 1), ("B", 5, 1), ("B", 4, 1), ("B", 7, 1)],
]
ORDER = [
    [("B", 0, 0), ("B", 0, 1), ("A", 3, 0), ("A", 2, 0), ("A", 1, 0), ("A", 1, 1),
     ("A", 3, 1), ("B", 3, 0), ("A", 6, 0), ("A", 2, 1), ("B", 2, 0), ("A", 5, 0)],
    [("A", 4, 0), ("B", 1, 0), ("B", 1, 1), ("B", 3, 1), ("A", 8, 0), ("A", 7, 0)],
    [("B", 6, 0), ("A", 6, 1)],
    [("B", 5, 0), ("B", 2, 1), ("B", 4, 0), ("A", 5, 1), ("B", 8, 0)],
    [("A", 4, 1), ("B", 7, 0)],
    [("A", 8, 1), ("B", 6, 1), ("A", 7, 1), ("B", 8, 1)],
    [("B", 5, 1), ("B", 4, 1), ("B", 7, 1)],
    [],
]


def signed(distance):
    return (distance,) if distance in (0, 8) else (-distance, distance)


SPOTS = []
for _block in BLOCKS:
    for _batch in _block:
        if _batch is None:
            SPOTS.append(None)
        else:
            SPOTS.extend(((_batch[0], r), _batch[2]) for r in signed(_batch[1]))
SPOTS += [(("A", 0), 0), (("A", 0), 1)]
PLACE = {spot: p for p, spot in enumerate(SPOTS) if spot is not None}
EMPTY = [p for p, spot in enumerate(SPOTS) if spot is None]
LAST = [
    [e for events in ORDER for e in events
     if any(((e[0], r), e[2]) in SPOTS[n:n + 4] for r in signed(e[1]))][-1]
    for n in range(0, SPANS, 4)
]
OVER_X = (1, 4, 5, 6)
ALONG = {0: (3, 2, 1), 3: (6, 5, 4)}


def kernel(q_ref, k_ref, v_ref, lens_in, order_in, out_ref,
           lens_ref, order_ref, buf, ext, qx, qtmp, vtmp, acc, top, send_sem, recv_sem, core_sem, local_sem):
    head = lax.axis_index("head")
    ctx = lax.axis_index("ctx")
    core = lax.rem(head, 2)
    y_lo = lax.rem(head // 2, 2)
    x_lo = ctx // RING
    z = lax.rem(ctx, RING)
    group = head // 4
    own = 2 * ctx
    other_x = 1 - x_lo

    local = [
        pltpu.make_async_copy(v_ref.at[group], vtmp, local_sem.at[0]),
        pltpu.make_async_copy(k_ref.at[group, y_lo], buf.at[0, 64], local_sem.at[1]),
        pltpu.make_async_copy(k_ref.at[group, 1 - y_lo], buf.at[0, 65], local_sem.at[2]),
        pltpu.make_async_copy(lens_in, lens_ref, local_sem.at[4]),
        pltpu.make_async_copy(order_in, order_ref, local_sem.at[5]),
        pltpu.make_async_copy(q_ref, qtmp, local_sem.at[3]),
    ]
    for copy in local:
        copy.start()

    for p in EMPTY:
        buf[0, p] = jnp.zeros((SPAN, DH), jnp.bfloat16)
        buf[1, p] = jnp.zeros((SPAN, DH), jnp.bfloat16)

    def along(distance):
        return {"ctx": x_lo * RING + lax.rem(z + distance + RING, RING)}

    to_x = {"ctx": other_x * RING + z}
    to_y = {"head": head + 2 - 4 * y_lo}
    to_core = {"head": head + 1 - 2 * core}

    barrier = pltpu.get_barrier_semaphore()
    for device in [along(d) for d in (1, -1, 2, -2, 3, -3)] + [to_x, to_y, to_core]:
        pl.semaphore_signal(barrier, inc=1, device_id=device, device_id_type=MESH)

    def unit(source, target, device):
        return pltpu.make_async_remote_copy(
            src_ref=buf.at[core, source],
            dst_ref=buf.at[core, target],
            send_sem=send_sem,
            recv_sem=recv_sem.at[target],
            device_id=device,
            device_id_type=MESH,
        )

    def pair(kv, n):
        return pltpu.make_async_remote_copy(
            src_ref=buf.at[kv, pl.ds(4 * n, 4)],
            dst_ref=buf.at[kv, pl.ds(4 * n, 4)],
            send_sem=send_sem,
            recv_sem=core_sem.at[n],
            device_id=to_core,
            device_id_type=MESH,
        )

    def send(source, target, device):
        unit(source, target, device).start()

    def relay(kind, distance, side):
        rels = signed(distance)
        here = [PLACE[(kind, r), side] for r in rels]
        for p in here:
            unit(p, p, to_core).wait_recv()
        if kind == "A":
            if distance == 6 and side == 0:
                up, down = PLACE[("A", -6), 0], PLACE[("A", 6), 0]
                send(up + core * (down - up), PLACE[("A", 8), 0], along(2 - 4 * core))
                for way in (1, -1):
                    send(PLACE[("A", -6 * way), 0], PLACE[("A", -7 * way), 0], along(way))
            if side == 0:
                for far in ALONG.get(distance, ()):
                    for way in (1, -1):
                        send(PLACE[("A", -way * distance), 0], PLACE[("A", -way * far), 0],
                             along(way * (far - distance)))
            if side == 0 or distance in OVER_X:
                for r, p in zip(rels, here):
                    send(p, PLACE[("B", r), side], to_x)
            if side == 0 and distance != 1:
                for r, p in zip(rels, here):
                    send(p, PLACE[("A", r), 1], to_y)
        elif side == 0 and distance and distance not in OVER_X:
            for r, p in zip(rels, here):
                send(p, PLACE[("B", r), 1], to_y)
        for n, event in enumerate(LAST):
            if event == (kind, distance, side):
                pair(core, n).start()

    def attend(keys, values, own_slot=False):
        values = jnp.concatenate(
            [values, jnp.ones((ONES, values.shape[1]), jnp.bfloat16)], axis=0
        )
        scores = jnp.dot(keys, qx[...], preferred_element_type=jnp.float32)
        if own_slot:
            key_row = lax.broadcasted_iota(jnp.int32, scores.shape, 0)
            query_row = lax.broadcasted_iota(jnp.int32, scores.shape, 1) % (2 * SPAN)
            later = (key_row > query_row) & ((key_row >= SPAN) == (query_row >= SPAN))
            scores = jnp.where(later, -BIG, scores)
        scores = scores * FACTOR
        highest = jnp.max(scores, axis=0, keepdims=True)
        if own_slot:
            new_top = highest
        else:
            old_top = top[0:1, :]
            new_top = jnp.maximum(old_top, highest)
        weights = jnp.exp2(scores - new_top).astype(jnp.bfloat16)
        mixed = jnp.dot(values, weights, preferred_element_type=jnp.float32)
        if own_slot:
            acc[...] = mixed
        else:
            acc[...] = acc[...] * jnp.exp2(old_top - new_top) + mixed
        top[0:1, :] = new_top

    local[0].wait()
    for j in (0, 1):
        block = vtmp[j].astype(jnp.float32)
        buf[1, 64 + (y_lo if j == 0 else 1 - y_lo)] = block.T.astype(jnp.bfloat16)
    local[1].wait()
    local[2].wait()
    pl.semaphore_wait(barrier, 9)
    for distance in ALONG[0]:
        for way in (1, -1):
            send(64, PLACE[("A", -way * distance), 0], along(way * distance))
    for side in (0, 1):
        send(64 + side, PLACE[("B", 0), side], to_x)
    for way in (1, -1):
        send(65, PLACE[("A", -way), 1], along(way))

    local[3].wait()
    local[4].wait()

    def borders(lane):
        opens = jnp.where(lane < SPANS, lane * SPAN, 1 << 20)
        closes = jnp.where(lane < SPANS, lane * SPAN + SPAN, 1 << 20)
        end = jnp.int32(0)
        for d in range(DOCS):
            opens = jnp.where(lane == SPANS + d, end, opens)
            end = end + lens_ref[d]
            closes = jnp.where(lane == SPANS + d, end if d < DOCS - 1 else 1 << 20, closes)
        return opens, closes

    lane = lax.broadcasted_iota(jnp.int32, (1, DH), 1)
    opens, closes = borders(lane)
    row = lax.broadcasted_iota(jnp.int32, (DH, 1), 0)
    row_opens, row_closes = borders(row)
    in_span = lax.broadcasted_iota(jnp.int32, (SPAN, 1), 0)

    for p, spot in enumerate(SPOTS):
        if spot is None:
            marks = jnp.where(lane == SPANS + DOCS, 1.0, 0.0) + jnp.zeros((SPAN, 1), jnp.float32)
        else:
            (kind, r), side = spot
            first = 2 * ((x_lo if kind == "A" else other_x) * RING + lax.rem(z + r + RING, RING))
            position = order_ref[first + (y_lo if side == 0 else 1 - y_lo)] * SPAN + in_span
            marks = jnp.where((position >= opens) & (position < closes), 1.0, 0.0)
        ext[p] = marks.astype(jnp.bfloat16)

    for j in (0, 1):
        position = order_ref[own + j] * SPAN + lax.broadcasted_iota(jnp.int32, (1, SPAN), 1)
        outside = jnp.where((position >= row_opens) & (position < row_closes), 0.0, -BIG)
        after = jnp.where(row > order_ref[own + j], -BIG, 0.0) + jnp.zeros((1, SPAN), jnp.float32)
        last = jnp.where(row == SPANS + DOCS, -BIG, 0.0) + jnp.zeros((1, SPAN), jnp.float32)
        side_q = jnp.where(row < SPANS, after, jnp.where(row < SPANS + DOCS, outside, last))
        for h in range(4):
            qx[DH:, (2 * h + j) * SPAN:(2 * h + j + 1) * SPAN] = side_q.astype(jnp.bfloat16)
    local[5].wait()
    for h in range(4):
        qx[:DH, 2 * h * SPAN:2 * (h + 1) * SPAN] = (
            qtmp[h].astype(jnp.float32).T.astype(jnp.bfloat16)
        )

    natural = [64 + y_lo, 65 - y_lo]
    attend(
        jnp.concatenate([jnp.concatenate([buf[0, p], ext[p]], axis=1) for p in natural], axis=0),
        jnp.concatenate([buf[1, p] for p in natural], axis=1),
        own_slot=True,
    )

    def turn(i, carry):
        for k, events in enumerate(ORDER):
            if events:
                @pl.when(i == k)
                def _():
                    for kind, distance, side in events:
                        relay(kind, distance, side)

        pair(1 - core, 2 * i).wait_recv()
        pair(1 - core, 2 * i + 1).wait_recv()
        eight = pl.ds(8 * i, 8)
        attend(
            jnp.concatenate(
                [buf[0, eight].reshape(8 * SPAN, DH), ext[eight].reshape(8 * SPAN, DH)], axis=1
            ),
            jnp.concatenate([buf[1, 8 * i + j] for j in range(8)], axis=1),
        )
        return carry

    lax.fori_loop(0, len(ORDER), turn, 0)

    result = acc[:DH, :] / acc[DH:DH + 1, :]
    for h in range(4):
        out_ref[h] = result[:, 2 * h * SPAN:2 * (h + 1) * SPAN].T.astype(jnp.bfloat16)
    pltpu.make_async_copy(buf.at[:, pl.ds(0, 63)], buf.at[:, pl.ds(0, 63)], send_sem).wait()


def body(queries, key_heads, value_heads, doc_lengths, span_order):
    heads, rows, _ = queries.shape
    shape = (key_heads.shape[0], 2, SPAN, DH)
    return pl.pallas_call(
        kernel,
        out_shape=jax.ShapeDtypeStruct(queries.shape, jnp.bfloat16),
        in_specs=[
            pl.BlockSpec(memory_space=pl.ANY),
            pl.BlockSpec(memory_space=pl.ANY),
            pl.BlockSpec(memory_space=pl.ANY),
            pl.BlockSpec(memory_space=pl.ANY),
            pl.BlockSpec(memory_space=pl.ANY),
        ],
        out_specs=pl.BlockSpec(memory_space=pltpu.VMEM),
        scratch_shapes=[
            pltpu.SMEM((DOCS,), jnp.int32),
            pltpu.SMEM((SPANS,), jnp.int32),
            pltpu.VMEM((2, SPANS + 2, SPAN, DH), jnp.bfloat16),
            pltpu.VMEM((SPANS + 2, SPAN, DH), jnp.bfloat16),
            pltpu.VMEM((2 * DH, heads * rows), jnp.bfloat16),
            pltpu.VMEM((heads, rows, DH), jnp.bfloat16),
            pltpu.VMEM((2, SPAN, DH), jnp.bfloat16),
            pltpu.VMEM((DH + ONES, heads * rows), jnp.float32),
            pltpu.VMEM((8, heads * rows), jnp.float32),
            pltpu.SemaphoreType.DMA,
            pltpu.SemaphoreType.DMA((SPANS,)),
            pltpu.SemaphoreType.DMA((SPANS // 4,)),
            pltpu.SemaphoreType.DMA((6,)),
        ],
        compiler_params=pltpu.CompilerParams(
            collective_id=0, has_side_effects=True, vmem_limit_bytes=54784 * 2**10
        ),
        cost_estimate=pl.CostEstimate(
            flops=4 * heads * rows * SPANS * SPAN * DH,
            bytes_accessed=2**20,
            transcendentals=heads * rows * SPANS * SPAN,
        ),
    )(queries, key_heads.reshape(shape), value_heads.reshape(shape), doc_lengths, span_order)


def solution(mesh):
    return jax.shard_map(
        body,
        mesh=mesh,
        in_specs=(P("head", "ctx", None), P(None, "ctx", None), P(None, "ctx", None), P(), P()),
        out_specs=P("head", "ctx", None),
        check_vma=False,
    )
```

```python
import math

import jax
import jax.numpy as jnp
from jax import lax
from jax.experimental import pallas as pl
from jax.experimental.pallas import tpu as pltpu
from jax.sharding import PartitionSpec as P

MESH = pl.DeviceIdType.MESH
SPAN = 128
DH = 128
DOCS = 16
SPANS = 64
RING = 16
BIG = 131072.0
FACTOR = math.log2(math.e) / math.sqrt(DH)
ONES = 16


BLOCKS = [
    [("B", 0, 0), ("B", 0, 1), ("A", 3, 0), ("A", 2, 0), ("A", 1, 0)],
    [("A", 1, 1), ("A", 3, 1), ("B", 3, 0), ("A", 6, 0)],
    [("A", 2, 1), ("B", 2, 0), ("A", 5, 0), ("A", 4, 0)],
    [("B", 1, 0), ("B", 1, 1), ("B", 3, 1), ("A", 8, 0), None],
    [("A", 7, 0), ("B", 6, 0), ("A", 6, 1), ("B", 5, 0)],
    [("B", 2, 1), ("B", 4, 0), ("A", 5, 1), ("B", 8, 0), None],
    [("A", 4, 1), ("B", 7, 0), ("A", 8, 1), ("B", 6, 1), ("B", 8, 1)],
    [("A", 7, 1), ("B", 5, 1), ("B", 4, 1), ("B", 7, 1)],
]
ORDER = [
    [("B", 0, 0), ("B", 0, 1), ("A", 3, 0), ("A", 2, 0), ("A", 1, 0), ("A", 1, 1),
     ("A", 3, 1), ("B", 3, 0), ("A", 6, 0), ("A", 2, 1), ("B", 2, 0), ("A", 5, 0)],
    [("A", 4, 0), ("B", 1, 0), ("B", 1, 1), ("B", 3, 1), ("A", 8, 0), ("A", 7, 0)],
    [("B", 6, 0), ("A", 6, 1)],
    [("B", 5, 0), ("B", 2, 1), ("B", 4, 0), ("A", 5, 1), ("B", 8, 0)],
    [("A", 4, 1), ("B", 7, 0)],
    [("A", 8, 1), ("B", 6, 1), ("A", 7, 1), ("B", 8, 1)],
    [("B", 5, 1), ("B", 4, 1), ("B", 7, 1)],
    [],
]


def signed(distance):
    return (distance,) if distance in (0, 8) else (-distance, distance)


SPOTS = []
for _block in BLOCKS:
    for _batch in _block:
        if _batch is None:
            SPOTS.append(None)
        else:
            SPOTS.extend(((_batch[0], r), _batch[2]) for r in signed(_batch[1]))
SPOTS += [(("A", 0), 0), (("A", 0), 1)]
PLACE = {spot: p for p, spot in enumerate(SPOTS) if spot is not None}
EMPTY = [p for p, spot in enumerate(SPOTS) if spot is None]
LAST = [
    [e for events in ORDER for e in events
     if any(((e[0], r), e[2]) in SPOTS[n:n + 4] for r in signed(e[1]))][-1]
    for n in range(0, SPANS, 4)
]
OVER_X = (1, 4, 5, 6)
ALONG = {0: (3, 2, 1), 3: (6, 5, 4)}


def kernel(q_ref, k_ref, v_ref, lens_in, order_in, out_ref,
           lens_ref, order_ref, buf, ext, qx, qtmp, vtmp, acc, top, send_sem, recv_sem, core_sem, local_sem):
    head = lax.axis_index("head")
    ctx = lax.axis_index("ctx")
    core = lax.rem(head, 2)
    y_lo = lax.rem(head // 2, 2)
    x_lo = ctx // RING
    z = lax.rem(ctx, RING)
    group = head // 4
    own = 2 * ctx
    other_x = 1 - x_lo

    local = [
        pltpu.make_async_copy(v_ref.at[group], vtmp, local_sem.at[0]),
        pltpu.make_async_copy(k_ref.at[group, y_lo], buf.at[0, 64], local_sem.at[1]),
        pltpu.make_async_copy(k_ref.at[group, 1 - y_lo], buf.at[0, 65], local_sem.at[2]),
        pltpu.make_async_copy(lens_in, lens_ref, local_sem.at[4]),
        pltpu.make_async_copy(order_in, order_ref, local_sem.at[5]),
        pltpu.make_async_copy(q_ref, qtmp, local_sem.at[3]),
    ]
    for copy in local:
        copy.start()

    for p in EMPTY:
        buf[0, p] = jnp.zeros((SPAN, DH), jnp.bfloat16)
        buf[1, p] = jnp.zeros((SPAN, DH), jnp.bfloat16)

    def along(distance):
        return {"ctx": x_lo * RING + lax.rem(z + distance + RING, RING)}

    to_x = {"ctx": other_x * RING + z}
    to_y = {"head": head + 2 - 4 * y_lo}
    to_core = {"head": head + 1 - 2 * core}

    barrier = pltpu.get_barrier_semaphore()
    for device in [along(d) for d in (1, -1, 2, -2, 3, -3)] + [to_x, to_y, to_core]:
        pl.semaphore_signal(barrier, inc=1, device_id=device, device_id_type=MESH)

    def unit(source, target, device):
        return pltpu.make_async_remote_copy(
            src_ref=buf.at[core, source],
            dst_ref=buf.at[core, target],
            send_sem=send_sem,
            recv_sem=recv_sem.at[target],
            device_id=device,
            device_id_type=MESH,
        )

    def pair(kv, n):
        return pltpu.make_async_remote_copy(
            src_ref=buf.at[kv, pl.ds(4 * n, 4)],
            dst_ref=buf.at[kv, pl.ds(4 * n, 4)],
            send_sem=send_sem,
            recv_sem=core_sem.at[n],
            device_id=to_core,
            device_id_type=MESH,
        )

    def send(source, target, device):
        unit(source, target, device).start()

    def relay(kind, distance, side):
        rels = signed(distance)
        here = [PLACE[(kind, r), side] for r in rels]
        for p in here:
            unit(p, p, to_core).wait_recv()
        if kind == "A":
            if distance == 6 and side == 0:
                up, down = PLACE[("A", -6), 0], PLACE[("A", 6), 0]
                send(up + core * (down - up), PLACE[("A", 8), 0], along(2 - 4 * core))
                for way in (1, -1):
                    send(PLACE[("A", -6 * way), 0], PLACE[("A", -7 * way), 0], along(way))
            if side == 0:
                for far in ALONG.get(distance, ()):
                    for way in (1, -1):
                        send(PLACE[("A", -way * distance), 0], PLACE[("A", -way * far), 0],
                             along(way * (far - distance)))
            if side == 0 or distance in OVER_X:
                for r, p in zip(rels, here):
                    send(p, PLACE[("B", r), side], to_x)
            if side == 0 and distance != 1:
                for r, p in zip(rels, here):
                    send(p, PLACE[("A", r), 1], to_y)
        elif side == 0 and distance and distance not in OVER_X:
            for r, p in zip(rels, here):
                send(p, PLACE[("B", r), 1], to_y)
        for n, event in enumerate(LAST):
            if event == (kind, distance, side):
                pair(core, n).start()

    def attend(keys, values, own_slot=False):
        values = jnp.concatenate(
            [values, jnp.ones((ONES, values.shape[1]), jnp.bfloat16)], axis=0
        )
        scores = jnp.dot(keys, qx[...], preferred_element_type=jnp.float32)
        if own_slot:
            key_row = lax.broadcasted_iota(jnp.int32, scores.shape, 0)
            query_row = lax.broadcasted_iota(jnp.int32, scores.shape, 1) % (2 * SPAN)
            later = (key_row > query_row) & ((key_row >= SPAN) == (query_row >= SPAN))
            scores = jnp.where(later, -BIG, scores)
        scores = scores * FACTOR
        highest = jnp.max(scores, axis=0, keepdims=True)
        if own_slot:
            new_top = highest
        else:
            old_top = top[0:1, :]
            new_top = jnp.maximum(old_top, highest)
        weights = jnp.exp2(scores - new_top).astype(jnp.bfloat16)
        mixed = jnp.dot(values, weights, preferred_element_type=jnp.float32)
        if own_slot:
            acc[...] = mixed
        else:
            acc[...] = acc[...] * jnp.exp2(old_top - new_top) + mixed
        top[0:1, :] = new_top

    def turned(side):
        block = vtmp[y_lo if side == 0 else 1 - y_lo].astype(jnp.float32)
        buf[1, 64 + side] = block.T.astype(jnp.bfloat16)

    local[0].wait()
    turned(0)
    local[1].wait()
    pl.semaphore_wait(barrier, 9)
    for distance in ALONG[0]:
        for way in (1, -1):
            send(64, PLACE[("A", -way * distance), 0], along(way * distance))
    send(64, PLACE[("B", 0), 0], to_x)
    turned(1)
    local[2].wait()
    send(65, PLACE[("B", 0), 1], to_x)
    for way in (1, -1):
        send(65, PLACE[("A", -way), 1], along(way))
    local[3].wait()
    local[4].wait()

    def borders(lane):
        opens = jnp.where(lane < SPANS, lane * SPAN, 1 << 20)
        closes = jnp.where(lane < SPANS, lane * SPAN + SPAN, 1 << 20)
        end = jnp.int32(0)
        for d in range(DOCS):
            opens = jnp.where(lane == SPANS + d, end, opens)
            end = end + lens_ref[d]
            closes = jnp.where(lane == SPANS + d, end if d < DOCS - 1 else 1 << 20, closes)
        return opens, closes

    lane = lax.broadcasted_iota(jnp.int32, (1, DH), 1)
    opens, closes = borders(lane)
    row = lax.broadcasted_iota(jnp.int32, (DH, 1), 0)
    row_opens, row_closes = borders(row)
    in_span = lax.broadcasted_iota(jnp.int32, (SPAN, 1), 0)

    for p, spot in enumerate(SPOTS):
        if spot is None:
            marks = jnp.where(lane == SPANS + DOCS, 1.0, 0.0) + jnp.zeros((SPAN, 1), jnp.float32)
        else:
            (kind, r), side = spot
            first = 2 * ((x_lo if kind == "A" else other_x) * RING + lax.rem(z + r + RING, RING))
            position = order_ref[first + (y_lo if side == 0 else 1 - y_lo)] * SPAN + in_span
            marks = jnp.where((position >= opens) & (position < closes), 1.0, 0.0)
        ext[p] = marks.astype(jnp.bfloat16)

    for j in (0, 1):
        position = order_ref[own + j] * SPAN + lax.broadcasted_iota(jnp.int32, (1, SPAN), 1)
        outside = jnp.where((position >= row_opens) & (position < row_closes), 0.0, -BIG)
        after = jnp.where(row > order_ref[own + j], -BIG, 0.0) + jnp.zeros((1, SPAN), jnp.float32)
        last = jnp.where(row == SPANS + DOCS, -BIG, 0.0) + jnp.zeros((1, SPAN), jnp.float32)
        side_q = jnp.where(row < SPANS, after, jnp.where(row < SPANS + DOCS, outside, last))
        for h in range(4):
            qx[DH:, (2 * h + j) * SPAN:(2 * h + j + 1) * SPAN] = side_q.astype(jnp.bfloat16)
    local[5].wait()
    for h in range(4):
        qx[:DH, 2 * h * SPAN:2 * (h + 1) * SPAN] = (
            qtmp[h].astype(jnp.float32).T.astype(jnp.bfloat16)
        )

    natural = [64 + y_lo, 65 - y_lo]
    attend(
        jnp.concatenate([jnp.concatenate([buf[0, p], ext[p]], axis=1) for p in natural], axis=0),
        jnp.concatenate([buf[1, p] for p in natural], axis=1),
        own_slot=True,
    )

    def turn(i, carry):
        for k, events in enumerate(ORDER):
            if events:
                @pl.when(i == k)
                def _():
                    for kind, distance, side in events:
                        relay(kind, distance, side)

        pair(1 - core, 2 * i).wait_recv()
        pair(1 - core, 2 * i + 1).wait_recv()
        eight = pl.ds(8 * i, 8)
        attend(
            jnp.concatenate(
                [buf[0, eight].reshape(8 * SPAN, DH), ext[eight].reshape(8 * SPAN, DH)], axis=1
            ),
            jnp.concatenate([buf[1, 8 * i + j] for j in range(8)], axis=1),
        )
        return carry

    lax.fori_loop(0, len(ORDER), turn, 0)

    result = acc[:DH, :] / acc[DH:DH + 1, :]
    for h in range(4):
        out_ref[h] = result[:, 2 * h * SPAN:2 * (h + 1) * SPAN].T.astype(jnp.bfloat16)
    pltpu.make_async_copy(buf.at[:, pl.ds(0, 63)], buf.at[:, pl.ds(0, 63)], send_sem).wait()


def body(queries, key_heads, value_heads, doc_lengths, span_order):
    heads, rows, _ = queries.shape
    shape = (key_heads.shape[0], 2, SPAN, DH)
    return pl.pallas_call(
        kernel,
        out_shape=jax.ShapeDtypeStruct(queries.shape, jnp.bfloat16),
        in_specs=[
            pl.BlockSpec(memory_space=pl.ANY),
            pl.BlockSpec(memory_space=pl.ANY),
            pl.BlockSpec(memory_space=pl.ANY),
            pl.BlockSpec(memory_space=pl.ANY),
            pl.BlockSpec(memory_space=pl.ANY),
        ],
        out_specs=pl.BlockSpec(memory_space=pltpu.VMEM),
        scratch_shapes=[
            pltpu.SMEM((DOCS,), jnp.int32),
            pltpu.SMEM((SPANS,), jnp.int32),
            pltpu.VMEM((2, SPANS + 2, SPAN, DH), jnp.bfloat16),
            pltpu.VMEM((SPANS + 2, SPAN, DH), jnp.bfloat16),
            pltpu.VMEM((2 * DH, heads * rows), jnp.bfloat16),
            pltpu.VMEM((heads, rows, DH), jnp.bfloat16),
            pltpu.VMEM((2, SPAN, DH), jnp.bfloat16),
            pltpu.VMEM((DH + ONES, heads * rows), jnp.float32),
            pltpu.VMEM((8, heads * rows), jnp.float32),
            pltpu.SemaphoreType.DMA,
            pltpu.SemaphoreType.DMA((SPANS,)),
            pltpu.SemaphoreType.DMA((SPANS // 4,)),
            pltpu.SemaphoreType.DMA((6,)),
        ],
        compiler_params=pltpu.CompilerParams(
            collective_id=0, has_side_effects=True, vmem_limit_bytes=54784 * 2**10
        ),
        cost_estimate=pl.CostEstimate(
            flops=4 * heads * rows * SPANS * SPAN * DH,
            bytes_accessed=2**20,
            transcendentals=heads * rows * SPANS * SPAN,
        ),
    )(queries, key_heads.reshape(shape), value_heads.reshape(shape), doc_lengths, span_order)


def solution(mesh):
    return jax.shard_map(
        body,
        mesh=mesh,
        in_specs=(P("head", "ctx", None), P(None, "ctx", None), P(None, "ctx", None), P(), P()),
        out_specs=P("head", "ctx", None),
        check_vma=False,
    )
```
